128 devices in a mesh: row: 8 (over z_lo, x), col: 16 (over y, z_hi, core).
Axes of the slice: x: 4, y: 4, z: 4 (z_hi: 2, z_lo: 2; z = z_hi * 2 + z_lo), core: 2. Of those that a mesh axis runs over, the one named last changes fastest.
Arguments:
- activations: bfloat16 [2, 256, 512, 256], P(None, 'row', 'col'), may hold values from -6 to 6
- cotangent: bfloat16 [2, 256, 512, 256], P(None, 'row', 'col'), may hold values from -6 to 6
- ln_gain: float32 [256], replicated, may hold values from 0.1 to 1.9
- qkv_weight: bfloat16 [256, 768], replicated, may hold values from -0.375 to 0.375
- out_weight: bfloat16 [256, 256], replicated, may hold values from -0.375 to 0.375
- position_bias: float32 [8, 64, 64], replicated, may hold values from -300 to 300
Outputs:
- grad_input: bfloat16 [2, 256, 512, 256], P(None, 'row', 'col')
- grad_gain: float32 [256], replicated
- grad_qkv: float32 [256, 768], replicated
- grad_proj: float32 [256, 256], replicated
- grad_bias: float32 [8, 64, 64], replicated
The draws below stay inside these ranges and needn't reach their ends.
All inputs are finite; a program needn't handle non-finite values.
Results may differ from the reference program's by a relative error of at most 0.01.
Values may be sent and summed in bfloat16 or wider, within the bound.
No kernel may reach another device: no remote copies, remote signals or barrier semaphores. Data moves between devices by JAX's collectives and lax.ppermute only.
A program may use at most 128 MiB of HBM per device.

```python
import math
import jax
import jax.numpy as jnp
from jax import lax

CHANNELS = 256
HEADS = 8
GRID = 8
GROUP = 64
BATCH = 2
MAP_ROWS = 256
MAP_COLS = 512


def draw_position_bias(key, part):
    key = jax.random.fold_in(key, 7)
    keys_list = jax.random.split(key, 1)
    shape = (HEADS, GROUP, GROUP)
    return jnp.clip(jax.random.normal(keys_list[0], shape, jnp.float32), -4.0, 4.0)


def shard_levels(rng, extent, cuts, smallest, top_value):
    def one(dim, shards_of):
        draws = jax.random.uniform(jax.random.fold_in(jax.random.fold_in(rng, 6), dim), (shards_of,), jnp.float32, smallest / len(cuts), top_value / len(cuts))
        return jnp.repeat(jnp.exp(draws), extent[dim] // shards_of).reshape((-1,) + (1,) * (len(extent) - dim - 1))

    loudness = one(*cuts[0])
    for cut in cuts[1:]:
        loudness = loudness * one(*cut)
    return loudness


def normal_values(rng, shape, scale, limit, pieces=(), kind=jnp.bfloat16):
    array = scale * jax.random.normal(rng, shape, jnp.float32)
    if pieces:
        array = array * shard_levels(rng, shape, pieces, -0.22, 0.18)
    return jnp.clip(array, -limit, limit).astype(kind)


def setup_inputs(seed: int = 0) -> dict:
    key_of = jax.random.split(jax.random.key(seed), 7)
    return {
        "activations": normal_values(key_of[0], (BATCH, MAP_ROWS, MAP_COLS, CHANNELS), 1.0, 6.0, ((1, 8), (2, 16))),
        "cotangent": normal_values(key_of[1], (BATCH, MAP_ROWS, MAP_COLS, CHANNELS), 1.0, 6.0, ((1, 8), (2, 16))),
        "ln_gain": jnp.clip(1.0 + 0.18 * jax.random.normal(key_of[2], (CHANNELS,), jnp.float32), 0.1, 1.9),
        "qkv_weight": normal_values(key_of[3], (CHANNELS, 3 * CHANNELS), CHANNELS ** -0.5, 0.375),
        "out_weight": normal_values(key_of[4], (CHANNELS, CHANNELS), CHANNELS ** -0.5, 0.375),
        "position_bias": draw_position_bias(jax.random.fold_in(key_of[6], 71), 0),
    }


def product(pattern, left_term, right_term):
    return jnp.einsum(pattern, left_term.astype(jnp.float32), right_term.astype(jnp.float32))

def layer_grads(x_groups, dy_groups, ln_gain, qkv_weight, out_weight, position_bias):
    groups, members, channels = x_groups.shape
    head_count = position_bias.shape[0]
    head_size = channels // head_count
    logit_scale = head_size ** (-0.5)
    x_float = x_groups.astype(jnp.float32)
    centred = x_float - lax.optimization_barrier(jnp.mean(x_float, axis=-1, keepdims=True))
    inverse = lax.rsqrt(lax.optimization_barrier(jnp.mean(centred * centred, axis=-1, keepdims=True)) + 1e-05)
    normal = centred * inverse
    normed = (normal * ln_gain).astype(jnp.bfloat16).reshape(groups * members, channels)
    packed = jnp.dot(normed, qkv_weight, preferred_element_type=jnp.float32).astype(jnp.bfloat16)
    packed = packed.reshape(groups, members, 3, head_count, head_size)
    queries, keys_part, values = (packed[:, :, 0], packed[:, :, 1], packed[:, :, 2])
    scores = product('gihd,gjhd->ghij', queries, keys_part) * logit_scale + position_bias[None]
    probabilities = jax.nn.softmax(scores, axis=-1)
    weights = probabilities.astype(jnp.bfloat16)
    attended = product('ghij,gjhd->gihd', weights, values).astype(jnp.bfloat16)
    attended = attended.reshape(groups * members, channels)
    upstream = dy_groups.reshape(groups * members, channels)
    grad_proj = jnp.dot(attended.T, upstream, preferred_element_type=jnp.float32)
    grad_attended = jnp.dot(upstream, out_weight.T, preferred_element_type=jnp.float32).astype(jnp.bfloat16)
    grad_attended = grad_attended.reshape(groups, members, head_count, head_size)
    grad_probs = product('gihd,gjhd->ghij', grad_attended, values)
    grad_values = product('ghij,gihd->gjhd', weights, grad_attended)
    grad_scores = probabilities * (grad_probs - lax.optimization_barrier(jnp.sum(grad_probs * probabilities, axis=-1, keepdims=True)))
    grad_bias = lax.optimization_barrier(jnp.sum(grad_scores, axis=0))
    scaled = (grad_scores * logit_scale).astype(jnp.bfloat16)
    grad_query = product('ghij,gjhd->gihd', scaled, keys_part)
    grad_keys = product('ghij,gihd->gjhd', scaled, queries)
    grad_packed = jnp.stack([grad_query, grad_keys, grad_values], axis=2).astype(jnp.bfloat16)
    grad_packed = grad_packed.reshape(groups * members, 3 * channels)
    grad_qkv = jnp.dot(normed.T, grad_packed, preferred_element_type=jnp.float32)
    grad_normed = jnp.dot(grad_packed, qkv_weight.T, preferred_element_type=jnp.float32)
    grad_normed = grad_normed.reshape(groups, members, channels)
    grad_gain = lax.optimization_barrier(jnp.sum(grad_normed * normal, axis=(0, 1)))
    grad_normal = grad_normed * ln_gain
    grad_input = dy_groups.astype(jnp.float32) + inverse * (grad_normal - lax.optimization_barrier(jnp.mean(grad_normal, axis=-1, keepdims=True)) - normal * lax.optimization_barrier(jnp.mean(grad_normal * normal, axis=-1, keepdims=True)))
    return (grad_input.astype(jnp.bfloat16), grad_gain, grad_qkv, grad_proj, grad_bias)

def to_groups(field):
    shaped = field.reshape(BATCH, GRID, MAP_ROWS // GRID, GRID, MAP_COLS // GRID, CHANNELS)
    return shaped.transpose(0, 2, 4, 1, 3, 5).reshape(-1, GROUP, CHANNELS)

def from_groups(field):
    shaped = field.reshape(BATCH, MAP_ROWS // GRID, MAP_COLS // GRID, GRID, GRID, CHANNELS)
    return shaped.transpose(0, 3, 1, 4, 2, 5).reshape(BATCH, MAP_ROWS, MAP_COLS, CHANNELS)

def reference(activations, cotangent, ln_gain, qkv_weight, out_weight, position_bias):
    group_total = BATCH * MAP_ROWS * MAP_COLS // GROUP
    block_size = math.gcd(group_total, 256)
    x_blocks = to_groups(activations).reshape(group_total // block_size, block_size, GROUP, CHANNELS)
    dy_blocks = to_groups(cotangent).reshape(group_total // block_size, block_size, GROUP, CHANNELS)

    def step_block(carry, pair):
        result = layer_grads(pair[0], pair[1], ln_gain, qkv_weight, out_weight, position_bias)
        summed = tuple((total_part + new_part for total_part, new_part in zip(carry, result[1:])))
        return (summed, result[0])
    initial = (jnp.zeros((CHANNELS,), jnp.float32), jnp.zeros((CHANNELS, 3 * CHANNELS), jnp.float32), jnp.zeros((CHANNELS, CHANNELS), jnp.float32), jnp.zeros((HEADS, GROUP, GROUP), jnp.float32))
    totals, grad_blocks = lax.scan(step_block, initial, (x_blocks, dy_blocks))
    grad_input = from_groups(grad_blocks.reshape(group_total, GROUP, CHANNELS))
    return (grad_input, totals[0], totals[1], totals[2], totals[3])
```

```python
import functools, math
import jax, jax.numpy as jnp
from jax import lax
from jax.experimental import pallas as pl
from jax.experimental.pallas import tpu as pltpu
from jax.sharding import PartitionSpec as P
F32=jnp.float32; BF=jnp.bfloat16
SC=32**-0.5; L2E=math.log2(math.e)
NT=(((1,),(1,)),((),())); TN=(((0,),(0,)),((),())); NN=(((1,),(0,)),((),()))
def dg(a,b,d): return lax.dot_general(a,b,d,preferred_element_type=F32)
def layer_kernel(NB,recv,gain,wqkv,wout,bias,msg,xf0,xf1,dyf0,dyf1,biasT,dbias,gqkv,gproj,ggain):
    def cvt(s,_):
        t=recv[s]
        for i,ref in enumerate((xf0,xf1,dyf0,dyf1)):
            ref[pl.ds(s*32,32),:]=t[:,128*i:128*i+128].astype(F32)
        return 0
    lax.fori_loop(0,64,cvt,0,unroll=8)
    for q in range(4):
        biasT[:,128*q:128*(q+1)]=(bias[128*q:128*(q+1),:]*L2E).T
    dbias[...]=jnp.zeros_like(dbias); gqkv[...]=jnp.zeros_like(gqkv); gproj[...]=jnp.zeros_like(gproj); ggain[...]=jnp.zeros_like(ggain)
    lane=lax.broadcasted_iota(jnp.int32,(64,128),1)//32
    masks=[lane==h for h in range(4)]
    zero=jnp.zeros((64,128),BF)
    def expand(a):
        return jnp.concatenate([jnp.where(m,a,zero) for m in masks],axis=0)
    def pick(r):
        o=r[0:64]
        for h in range(1,4): o=jnp.where(masks[h],r[64*h:64*h+64],o)
        return o
    w=wqkv[...]; wo=wout[...]; gn=gain[...]
    def block(b,_):
        def grouped(lo,hi):
            return jnp.concatenate([jnp.concatenate([ref[pl.ds(b*NB+k,64,stride=32),:] for k in range(NB)],0) for ref in (lo,hi)],1)
        x=grouped(xf0,xf1); dy=grouped(dyf0,dyf1)
        c=x-jnp.mean(x,-1,keepdims=True)
        inv=lax.rsqrt(jnp.mean(c*c,-1,keepdims=True)+1e-5)
        normal=c*inv
        normed=(normal*gn).astype(BF)
        packed=dg(normed,w,NN)
        Q=(packed[:,:256]*(SC*L2E)).astype(BF); K=packed[:,256:512].astype(BF); V=packed[:,512:].astype(BF)
        dyb=dy.astype(BF)
        dA=dg(dyb,wo,NT).astype(BF)
        att=[];gp=[];db=[None,None]
        for k in range(NB):
            r=slice(64*k,64*k+64)
            aH=[];gq=[];gk=[];gv=[]
            for hf in range(2):
                l=slice(128*hf,128*hf+128)
                q=Q[r,l];kk=K[r,l];v=V[r,l];da=dA[r,l]
                qx=expand(q);dax=expand(da)
                t=dg(kk,qx,NT)+biasT[:,256*hf:256*hf+256]
                m=jnp.max(t,0,keepdims=True)
                e=jnp.exp2(t-m)
                p=e*(1.0/jnp.sum(e,0,keepdims=True))
                pb=p.astype(BF)
                dp=dg(v,dax,NT)
                D=jnp.sum(dp*p,0,keepdims=True)
                s=p*(dp-D)
                sb=s.astype(BF)
                db[hf]=s if db[hf] is None else db[hf]+s
                aH.append(pick(dg(pb,v,TN)).astype(BF))
                gv.append(dg(pb,dax,NN).astype(BF))
                gk.append((dg(sb,qx,NN)*(1.0/L2E)).astype(BF))
                gq.append((pick(dg(sb,kk,TN))*SC).astype(BF))
            att.append(jnp.concatenate(aH,1))
            gp.append(jnp.concatenate(gq+gk+gv,1))
        for hf in range(2): dbias[:,256*hf:256*hf+256]+=db[hf]
        A=jnp.concatenate(att,0); G=jnp.concatenate(gp,0)
        gqkv[...]+=dg(normed,G,TN)
        gproj[...]+=dg(A,dyb,TN)
        gN=dg(G,w,NT)
        gx=gN*normal
        ggain[...]+=jnp.sum(gx.reshape(-1,8,256),0)
        g=gN*gn
        dx=dy+inv*(g-jnp.mean(g,-1,keepdims=True)-normal*jnp.mean(gx*gn,-1,keepdims=True))
        for k in range(NB):
            xf0[pl.ds(b*NB+k,64,stride=32),:]=dx[64*k:64*k+64,:128]
            xf1[pl.ds(b*NB+k,64,stride=32),:]=dx[64*k:64*k+64,128:]
        return 0
    lax.fori_loop(0,32//NB,block,0)
    def wr(s,_):
        for i,ref in enumerate((xf0,xf1)):
            t=ref[pl.ds(s*32,32),:].astype(BF)
            msg[s,:,128*i:128*i+128]=t[:16]
            msg[s,:,256+128*i:384+128*i]=t[16:]
        return 0
    lax.fori_loop(0,64,wr,0,unroll=8)
    for rb in range(16):
        rr=slice(16*rb,16*rb+16)
        msg[rb*3,:,512:896]=gqkv[rr,0:384].astype(BF)
        msg[rb*3+1,:,512:896]=gqkv[rr,384:768].astype(BF)
        msg[rb*3+2,:,512:768]=gproj[rr,:].astype(BF)
        q=rb//4; j0=16*(rb%4)
        msg[rb*3+2,:,768:896]=dbias[j0:j0+16,128*q:128*q+128].astype(BF)
    msg[48:64,:,512:896]=jnp.zeros((16,16,384),BF)
    gs=jnp.sum(ggain[...],0,keepdims=True)
    msg[48,:,512:768]=jnp.broadcast_to(gs,(16,256)).astype(BF)
def layer(recv,gain,wqkv,wout,bias,NB=4):
    vm=pl.BlockSpec(memory_space=pltpu.VMEM)
    return pl.pallas_call(functools.partial(layer_kernel,NB),
        out_shape=jax.ShapeDtypeStruct((64,16,896),BF),
        in_specs=[vm]*5,out_specs=vm,
        scratch_shapes=[*[pltpu.VMEM((2048,128),F32)]*4,pltpu.VMEM((64,512),F32),pltpu.VMEM((64,512),F32),
            pltpu.VMEM((256,768),F32),pltpu.VMEM((256,256),F32),pltpu.VMEM((8,256),F32)],
        compiler_params=pltpu.CompilerParams(vmem_limit_bytes=48*2**20),
        name="grid_attention_grads")(recv,gain.reshape(1,256),wqkv,wout,bias.reshape(512,64))


def finish_kernel(y, qkv, proj, bias, gain):
    for rb in range(16):
        rr = slice(16 * rb, 16 * rb + 16)
        qkv[rr, 0:384] = y[rb * 3].astype(F32)
        qkv[rr, 384:768] = y[rb * 3 + 1].astype(F32)
        proj[rr, :] = y[rb * 3 + 2, :, 0:256].astype(F32)
    for q in range(4):
        t = jnp.concatenate([y[(q * 4 + r) * 3 + 2, :, 256:384].astype(F32) for r in range(4)], 0)
        bias[128 * q : 128 * q + 128, :] = t.T
    gain[...] = y[48, 0:1, 0:256].astype(F32)


def finish(y):
    vm = pl.BlockSpec(memory_space=pltpu.VMEM)
    return pl.pallas_call(
        finish_kernel,
        out_shape=(
            jax.ShapeDtypeStruct((256, 768), F32),
            jax.ShapeDtypeStruct((256, 256), F32),
            jax.ShapeDtypeStruct((512, 64), F32),
            jax.ShapeDtypeStruct((1, 256), F32),
        ),
        in_specs=[vm],
        out_specs=(vm,) * 4,
        name="parameter_grads",
    )(y)


CHIPS = ("zl", "x", "y", "zh")


def on_device(activations, cotangent, ln_gain, qkv_weight, out_weight, position_bias):
    both = jnp.concatenate(
        [activations.reshape(64, 32, 256), cotangent.reshape(64, 32, 256)], axis=2
    )
    arrived = lax.all_to_all(both, CHIPS, 0, 0, tiled=True)
    message = layer(arrived, ln_gain, qkv_weight, out_weight, position_bias)
    returned = lax.all_to_all(message, CHIPS, 0, 0, tiled=True)
    partial = jnp.sum(returned[:, :, 512:].astype(F32), axis=0)
    other = lax.ppermute(partial, "core", [(0, 1), (1, 0)])
    total = jnp.broadcast_to((partial + other).astype(BF)[None], (64, 16, 384))
    totals = lax.all_to_all(total, CHIPS, 0, 0, tiled=True)
    grad_input = returned[:, :, :512].reshape(64, 16, 2, 256).transpose(0, 2, 1, 3)
    grad_input = grad_input.reshape(activations.shape)
    grad_qkv, grad_proj, grad_bias, grad_gain = finish(totals)
    return (
        grad_input,
        grad_gain.reshape(256),
        grad_qkv,
        grad_proj,
        grad_bias.reshape(8, 64, 64),
    )


def solution(mesh):
    fine = jax.sharding.Mesh(mesh.devices.reshape(2, 4, 4, 2, 2), ("zl", "x", "y", "zh", "core"))
    tokens = P(None, ("zl", "x"), ("y", "zh", "core"), None)
    return jax.shard_map(
        on_device,
        mesh=fine,
        in_specs=(tokens, tokens, P(), P(), P(), P()),
        out_specs=(tokens, P(), P(), P(), P()),
        check_vma=False,
    )
```

```python
import functools, math
import jax, jax.numpy as jnp
from jax import lax
from jax.experimental import pallas as pl
from jax.experimental.pallas import tpu as pltpu
from jax.sharding import PartitionSpec as P
F32=jnp.float32; BF=jnp.bfloat16
SC=32**-0.5; L2E=math.log2(math.e)
NT=(((1,),(1,)),((),())); TN=(((0,),(0,)),((),())); NN=(((1,),(0,)),((),()))
ST=40
def dg(a,b,d): return lax.dot_general(a,b,d,preferred_element_type=F32)
def attention(NB,Q,K,V,dA,biasT,expand,pick):
    units=[(k,hf) for k in range(NB) for hf in range(2)]
    def sl(a,k,hf): return a[64*k:64*k+64,128*hf:128*hf+128]
    qx={};dax={};t={};dp={};pb={};sb={};o={}
    db=[None]*2
    ch=2*NB
    for c0 in range(0,len(units),ch):
        us=units[c0:c0+ch]
        for u in us:
            qx[u]=expand(sl(Q,*u)); dax[u]=expand(sl(dA,*u))
            t[u]=dg(sl(K,*u),qx[u],NT); dp[u]=dg(sl(V,*u),dax[u],NT)
        for u in us:
            hf=u[1]
            x=t[u]+biasT[:,256*hf:256*hf+256]
            m=jnp.max(x,0,keepdims=True)
            e=jnp.exp2(x-m)
            p=e*(1.0/jnp.sum(e,0,keepdims=True))
            pb[u]=p.astype(BF)
            D=jnp.sum(dp[u]*p,0,keepdims=True)
            s=p*(dp[u]-D)
            sb[u]=s.astype(BF)
            db[hf]=s if db[hf] is None else db[hf]+s
        for u in us:
            o[u]=(pick(dg(pb[u],sl(V,*u),TN)).astype(BF),dg(pb[u],dax[u],NN).astype(BF),
                  (dg(sb[u],qx[u],NN)*(1.0/L2E)).astype(BF),(pick(dg(sb[u],sl(K,*u),TN))*SC).astype(BF))
    return o,db
def layer_kernel(NB,recv,gain,wqkv,wout,bias,msg,xf0,xf1,dyf0,dyf1,biasT,dbias,ggain,nrm,inv_s,nS,qS,kS,vS,daS,dS,aS,gS):
    def cvt(s,_):
        t=recv[s]
        for i,ref in enumerate((xf0,xf1,dyf0,dyf1)):
            ref[pl.ds(s*ST,32),:]=t[:,128*i:128*i+128].astype(F32)
        return 0
    lax.fori_loop(0,64,cvt,0,unroll=8)
    for q in range(4):
        biasT[:,128*q:128*(q+1)]=(bias[128*q:128*(q+1),:]*L2E).T
    dbias[...]=jnp.zeros_like(dbias); ggain[...]=jnp.zeros_like(ggain)
    lane=lax.broadcasted_iota(jnp.int32,(64,128),1)//32
    masks=[lane==h for h in range(4)]
    zero=jnp.zeros((64,128),BF)
    def expand(a):
        return jnp.concatenate([jnp.where(m,a,zero) for m in masks],axis=0)
    def pick(r):
        o=r[0:64]
        for h in range(1,4): o=jnp.where(masks[h],r[64*h:64*h+64],o)
        return o
    w=wqkv[...]; wo=wout[...]; gn=gain[...]
    PA=8; RA=64*PA
    def phase_a(b,_):
        def grouped(lo,hi):
            return jnp.concatenate([jnp.concatenate([ref[pl.ds(b*PA+k,64,stride=ST),:] for k in range(PA)],0) for ref in (lo,hi)],1)
        rr=pl.ds(pl.multiple_of(b*RA,RA),RA)
        x=grouped(xf0,xf1); dyb=grouped(dyf0,dyf1).astype(BF)
        dS[rr,:]=dyb
        daS[rr,:]=dg(dyb,wo,NT).astype(BF)
        c=x-jnp.mean(x,-1,keepdims=True)
        inv=lax.rsqrt(jnp.mean(c*c,-1,keepdims=True)+1e-5)
        normal=c*inv
        nrm[rr,:]=normal; inv_s[rr,:]=jnp.broadcast_to(inv,(RA,128))
        normed=(normal*gn).astype(BF)
        nS[rr,:]=normed
        packed=dg(normed,w,NN)
        qS[rr,:]=(packed[:,:256]*(SC*L2E)).astype(BF); kS[rr,:]=packed[:,256:512].astype(BF); vS[rr,:]=packed[:,512:].astype(BF)
        return 0
    lax.fori_loop(0,32//PA,phase_a,0,unroll=4)
    RB=64*NB
    def phase_b(b,_):
        rr=pl.ds(pl.multiple_of(b*RB,RB),RB)
        o,db=attention(NB,qS[rr,:],kS[rr,:],vS[rr,:],daS[rr,:],biasT,expand,pick)
        for k in range(NB):
            r=pl.ds(pl.multiple_of(b*RB+64*k,64),64)
            for hf in range(2):
                a,gv,gk,gq=o[(k,hf)]
                l=slice(128*hf,128*hf+128)
                aS[r,l]=a
                gS[r,128*hf:128*hf+128]=gq; gS[r,256+128*hf:384+128*hf]=gk; gS[r,512+128*hf:640+128*hf]=gv
        for hf in range(2): dbias[:,256*hf:256*hf+256]+=db[hf]
        return 0
    lax.fori_loop(0,32//NB,phase_b,0,unroll=1)
    PC=8; RC=64*PC
    def phase_c(b,_):
        rr=pl.ds(pl.multiple_of(b*RC,RC),RC)
        gN=dg(gS[rr,:],w,NT)
        normal=nrm[rr,:]
        i1=inv_s[rr,:]; inv=jnp.concatenate([i1,i1],1)
        gx=gN*normal
        ggain[...]+=jnp.sum(gx.reshape(-1,8,256),0)
        g=gN*gn
        dx=dS[rr,:].astype(F32)+inv*(g-jnp.mean(g,-1,keepdims=True)-normal*jnp.mean(gx*gn,-1,keepdims=True))
        for k in range(PC):
            xf0[pl.ds(b*PC+k,64,stride=ST),:]=dx[64*k:64*k+64,:128]
            xf1[pl.ds(b*PC+k,64,stride=ST),:]=dx[64*k:64*k+64,128:]
        return 0
    lax.fori_loop(0,32//PC,phase_c,0,unroll=4)
    gqkv=dg(nS[...],gS[...],TN).astype(BF)
    gproj=dg(aS[...],dS[...],TN).astype(BF)
    for rb in range(16):
        rr=slice(16*rb,16*rb+16)
        msg[rb*3,:,512:896]=gqkv[rr,0:384]
        msg[rb*3+1,:,512:896]=gqkv[rr,384:768]
        msg[rb*3+2,:,512:768]=gproj[rr,:]
        q=rb//4; j0=16*(rb%4)
        msg[rb*3+2,:,768:896]=dbias[j0:j0+16,128*q:128*q+128].astype(BF)
    def wr(s,_):
        for i,ref in enumerate((xf0,xf1)):
            t=ref[pl.ds(s*ST,32),:].astype(BF)
            msg[s,:,128*i:128*i+128]=t[:16]
            msg[s,:,256+128*i:384+128*i]=t[16:]
        return 0
    lax.fori_loop(0,64,wr,0,unroll=8)
    msg[48:64,:,512:896]=jnp.zeros((16,16,384),BF)
    gs=jnp.sum(ggain[...],0,keepdims=True)
    msg[48,:,512:768]=jnp.broadcast_to(gs,(16,256)).astype(BF)
def layer(recv,gain,wqkv,wout,bias,NB=8):
    vm=pl.BlockSpec(memory_space=pltpu.VMEM)
    return pl.pallas_call(functools.partial(layer_kernel,NB),
        out_shape=jax.ShapeDtypeStruct((64,16,896),BF),
        in_specs=[vm]*5,out_specs=vm,
        scratch_shapes=[*[pltpu.VMEM((64*ST,128),F32)]*4,pltpu.VMEM((64,512),F32),pltpu.VMEM((64,512),F32),pltpu.VMEM((8,256),F32),
            pltpu.VMEM((2048,256),F32),pltpu.VMEM((2048,128),F32),*[pltpu.VMEM((2048,256),BF)]*7,pltpu.VMEM((2048,768),BF)],
        compiler_params=pltpu.CompilerParams(vmem_limit_bytes=48*2**20),
        name="grid_attention_grads")(recv,gain.reshape(1,256),wqkv,wout,bias.reshape(512,64))


def finish_kernel(y, qkv, proj, bias, gain):
    for rb in range(16):
        rr = slice(16 * rb, 16 * rb + 16)
        qkv[rr, 0:384] = y[rb * 3].astype(F32)
        qkv[rr, 384:768] = y[rb * 3 + 1].astype(F32)
        proj[rr, :] = y[rb * 3 + 2, :, 0:256].astype(F32)
    for q in range(4):
        t = jnp.concatenate([y[(q * 4 + r) * 3 + 2, :, 256:384].astype(F32) for r in range(4)], 0)
        bias[128 * q : 128 * q + 128, :] = t.T
    gain[...] = y[48, 0:1, 0:256].astype(F32)


def finish(y):
    vm = pl.BlockSpec(memory_space=pltpu.VMEM)
    return pl.pallas_call(
        finish_kernel,
        out_shape=(
            jax.ShapeDtypeStruct((256, 768), F32),
            jax.ShapeDtypeStruct((256, 256), F32),
            jax.ShapeDtypeStruct((512, 64), F32),
            jax.ShapeDtypeStruct((1, 256), F32),
        ),
        in_specs=[vm],
        out_specs=(vm,) * 4,
        name="parameter_grads",
    )(y)


CHIPS = ("zl", "x", "y", "zh")


def on_device(activations, cotangent, ln_gain, qkv_weight, out_weight, position_bias):
    both = jnp.concatenate(
        [activations.reshape(64, 32, 256), cotangent.reshape(64, 32, 256)], axis=2
    )
    arrived = lax.all_to_all(both, CHIPS, 0, 0, tiled=True)
    message = layer(arrived, ln_gain, qkv_weight, out_weight, position_bias)
    returned = lax.all_to_all(message, CHIPS, 0, 0, tiled=True)
    partial = jnp.sum(returned[:, :, 512:].astype(F32), axis=0)
    other = lax.ppermute(partial, "core", [(0, 1), (1, 0)])
    total = jnp.broadcast_to((partial + other).astype(BF)[None], (64, 16, 384))
    totals = lax.all_to_all(total, CHIPS, 0, 0, tiled=True)
    grad_input = returned[:, :, :512].reshape(64, 16, 2, 256).transpose(0, 2, 1, 3)
    grad_input = grad_input.reshape(activations.shape)
    grad_qkv, grad_proj, grad_bias, grad_gain = finish(totals)
    return (
        grad_input,
        grad_gain.reshape(256),
        grad_qkv,
        grad_proj,
        grad_bias.reshape(8, 64, 64),
    )


def solution(mesh):
    fine = jax.sharding.Mesh(mesh.devices.reshape(2, 4, 4, 2, 2), ("zl", "x", "y", "zh", "core"))
    tokens = P(None, ("zl", "x"), ("y", "zh", "core"), None)
    return jax.shard_map(
        on_device,
        mesh=fine,
        in_specs=(tokens, tokens, P(), P(), P(), P()),
        out_specs=(tokens, P(), P(), P(), P()),
        check_vma=False,
    )
```

```python
import functools
import math

import jax
import jax.numpy as jnp
from jax import lax
from jax.experimental import pallas as pl
from jax.experimental.pallas import tpu as pltpu
from jax.sharding import PartitionSpec as P

F32 = jnp.float32
BF = jnp.bfloat16
MEMBERS = 64
GROUPS = 32
TOKENS = MEMBERS * GROUPS
STRIDE = 40
SCALE = 32**-0.5
LOG2E = math.log2(math.e)
NN = (((1,), (0,)), ((), ()))
NT = (((1,), (1,)), ((), ()))
TN = (((0,), (0,)), ((), ()))
CHIPS = ("zl", "x", "y", "zh")
VM = pl.BlockSpec(memory_space=pltpu.VMEM)
HBM = pl.BlockSpec(memory_space=pltpu.HBM)
MIB = 2**20


def dot(a, b, dims):
    return lax.dot_general(a, b, dims, preferred_element_type=F32)


def unpack(recv, refs):
    def step(s, _):
        rows = recv[s]
        for i, ref in enumerate(refs):
            ref[pl.ds(s * STRIDE, GROUPS), :] = rows[:, 128 * i : 128 * i + 128].astype(F32)
        return 0

    lax.fori_loop(0, MEMBERS, step, 0, unroll=8)


def grouped(refs, first, count):
    columns = [
        jnp.concatenate(
            [ref[pl.ds(first + k, MEMBERS, stride=STRIDE), :] for k in range(count)], axis=0
        )
        for ref in refs
    ]
    return jnp.concatenate(columns, axis=1)


def normalise(x):
    centred = x - jnp.mean(x, -1, keepdims=True)
    inverse = lax.rsqrt(jnp.mean(centred * centred, -1, keepdims=True) + 1e-5)
    return centred * inverse, inverse


def head_masks():
    lane = lax.broadcasted_iota(jnp.int32, (MEMBERS, 128), 1) // 32
    return [lane == h for h in range(4)]


def expand(a, masks):
    zero = jnp.zeros_like(a)
    return jnp.concatenate([jnp.where(m, a, zero) for m in masks], axis=0)


def pick(r, masks):
    out = r[0:MEMBERS]
    for h in range(1, 4):
        out = jnp.where(masks[h], r[MEMBERS * h : MEMBERS * (h + 1)], out)
    return out


def attention(count, q, k, v, da, bias, masks):
    units = [(g, hf) for g in range(count) for hf in range(2)]

    def part(a, u):
        g, hf = u
        return a[MEMBERS * g : MEMBERS * (g + 1), 128 * hf : 128 * (hf + 1)]

    qx = {u: expand(part(q, u), masks) for u in units}
    dax = {u: expand(part(da, u), masks) for u in units}
    scores = {}
    grad_probs = {}
    for u in units:
        scores[u] = dot(part(k, u), qx[u], NT)
        grad_probs[u] = dot(part(v, u), dax[u], NT)
    weights = {}
    scaled = {}
    grad_bias = [None, None]
    for u in units:
        hf = u[1]
        logits = scores[u] + bias[:, 256 * hf : 256 * (hf + 1)]
        e = jnp.exp2(logits - jnp.max(logits, 0, keepdims=True))
        p = e * (1.0 / jnp.sum(e, 0, keepdims=True))
        ds = p * (grad_probs[u] - jnp.sum(grad_probs[u] * p, 0, keepdims=True))
        weights[u] = p.astype(BF)
        scaled[u] = ds.astype(BF)
        grad_bias[hf] = ds if grad_bias[hf] is None else grad_bias[hf] + ds
    results = {}
    for u in units:
        attended = pick(dot(weights[u], part(v, u), TN), masks)
        grad_v = dot(weights[u], dax[u], NN)
        grad_k = dot(scaled[u], qx[u], NN) * (1.0 / LOG2E)
        grad_q = pick(dot(scaled[u], part(k, u), TN), masks) * SCALE
        results[u] = [r.astype(BF) for r in (attended, grad_q, grad_k, grad_v)]
    return results, grad_bias


def gradients_kernel(
    recv, gain, wqkv, wout, bias, msg, grad_packed,
    x0, x1, d0, d1, bias_t, grad_bias, normed_s, q_s, k_s, v_s, da_s, dy_s, att_s, gp_s, sem,
):
    unpack(recv, (x0, x1, d0, d1))
    for t in range(4):
        bias_t[:, 128 * t : 128 * (t + 1)] = (bias[128 * t : 128 * (t + 1), :] * LOG2E).T
    grad_bias[...] = jnp.zeros_like(grad_bias)
    masks = head_masks()

    def project(b, _):
        rows = pl.ds(pl.multiple_of(b * 512, 512), 512)
        dy = grouped((d0, d1), b * 8, 8).astype(BF)
        dy_s[rows, :] = dy
        da_s[rows, :] = dot(dy, wout[...], NT).astype(BF)
        normal, _ = normalise(grouped((x0, x1), b * 8, 8))
        normed = (normal * gain[...]).astype(BF)
        normed_s[rows, :] = normed
        packed = dot(normed, wqkv[...], NN)
        q_s[rows, :] = (packed[:, :256] * (SCALE * LOG2E)).astype(BF)
        k_s[rows, :] = packed[:, 256:512].astype(BF)
        v_s[rows, :] = packed[:, 512:].astype(BF)
        return 0

    lax.fori_loop(0, GROUPS // 8, project, 0, unroll=4)

    def attend(b, _):
        rows = pl.ds(pl.multiple_of(b * 512, 512), 512)
        results, gb = attention(
            8, q_s[rows, :], k_s[rows, :], v_s[rows, :], da_s[rows, :], bias_t, masks
        )
        for (g, hf), (att, gq, gk, gv) in results.items():
            r = pl.ds(pl.multiple_of(b * 512 + MEMBERS * g, MEMBERS), MEMBERS)
            att_s[r, 128 * hf : 128 * (hf + 1)] = att
            for i, part in enumerate((gq, gk, gv)):
                gp_s[r, 256 * i + 128 * hf : 256 * i + 128 * (hf + 1)] = part
        for hf in range(2):
            grad_bias[:, 256 * hf : 256 * (hf + 1)] += gb[hf]
        return 0

    lax.fori_loop(0, GROUPS // 8, attend, 0)
    copy = pltpu.make_async_copy(gp_s, grad_packed, sem)
    copy.start()
    grad_qkv = dot(normed_s[...], gp_s[...], TN).astype(BF)
    grad_proj = dot(att_s[...], dy_s[...], TN).astype(BF)
    for rb in range(16):
        rr = slice(16 * rb, 16 * rb + 16)
        t, j = rb // 4, 16 * (rb % 4)
        msg[3 * rb] = grad_qkv[rr, 0:384]
        msg[3 * rb + 1] = grad_qkv[rr, 384:768]
        msg[3 * rb + 2, :, 0:256] = grad_proj[rr, :]
        msg[3 * rb + 2, :, 256:384] = grad_bias[j : j + 16, 128 * t : 128 * (t + 1)].astype(BF)
    msg[48:64] = jnp.zeros((16, 16, 384), BF)
    copy.wait()


def gradients(recv, gain, wqkv, wout, bias):
    return pl.pallas_call(
        gradients_kernel,
        out_shape=(
            jax.ShapeDtypeStruct((64, 16, 384), BF),
            jax.ShapeDtypeStruct((TOKENS, 768), BF),
        ),
        in_specs=[VM] * 5,
        out_specs=(VM, HBM),
        scratch_shapes=[
            *[pltpu.VMEM((MEMBERS * STRIDE, 128), F32)] * 4,
            *[pltpu.VMEM((MEMBERS, 512), F32)] * 2,
            *[pltpu.VMEM((TOKENS, 256), BF)] * 7,
            pltpu.VMEM((TOKENS, 768), BF),
            pltpu.SemaphoreType.DMA,
        ],
        compiler_params=pltpu.CompilerParams(vmem_limit_bytes=50 * MIB),
        cost_estimate=pl.CostEstimate(
            flops=8 * 10**9, bytes_accessed=8 * 2**20, transcendentals=8 * 2**20
        ),
        name="parameter_gradients",
    )(recv, gain, wqkv, wout, bias)


def input_kernel(recv, grad_packed, gain, wqkv, out, x0, x1, d0, d1, gp_s, sem):
    copy = pltpu.make_async_copy(grad_packed, gp_s, sem)
    copy.start()
    unpack(recv, (x0, x1, d0, d1))
    copy.wait()

    def block(b, _):
        rows = pl.ds(pl.multiple_of(b * 512, 512), 512)
        g = dot(gp_s[rows, :], wqkv[...], NT) * gain[...]
        normal, inverse = normalise(grouped((x0, x1), b * 8, 8))
        along = jnp.mean(g * normal, -1, keepdims=True)
        dx = inverse * (g - jnp.mean(g, -1, keepdims=True) - normal * along)
        dx = grouped((d0, d1), b * 8, 8) + dx
        for k in range(8):
            for i, ref in enumerate((x0, x1)):
                ref[pl.ds(b * 8 + k, MEMBERS, stride=STRIDE), :] = dx[
                    MEMBERS * k : MEMBERS * (k + 1), 128 * i : 128 * (i + 1)
                ]
        return 0

    lax.fori_loop(0, GROUPS // 8, block, 0, unroll=4)

    def write(s, _):
        for i, ref in enumerate((x0, x1)):
            rows = ref[pl.ds(s * STRIDE, GROUPS), :].astype(BF)
            out[s, :, 128 * i : 128 * i + 128] = rows[:16]
            out[s, :, 256 + 128 * i : 384 + 128 * i] = rows[16:]
        return 0

    lax.fori_loop(0, MEMBERS, write, 0, unroll=8)


def input_gradient(recv, grad_packed, gain, wqkv):
    return pl.pallas_call(
        input_kernel,
        out_shape=jax.ShapeDtypeStruct((64, 16, 512), BF),
        in_specs=[VM, HBM, VM, VM],
        out_specs=VM,
        scratch_shapes=[
            *[pltpu.VMEM((MEMBERS * STRIDE, 128), F32)] * 4,
            pltpu.VMEM((TOKENS, 768), BF),
            pltpu.SemaphoreType.DMA,
        ],
        compiler_params=pltpu.CompilerParams(vmem_limit_bytes=50 * MIB),
        cost_estimate=pl.CostEstimate(
            flops=6 * 10**9, bytes_accessed=16 * 2**20, transcendentals=2**20
        ),
        name="input_gradient",
    )(recv, grad_packed, gain, wqkv)


def spread_kernel(mine, other, dx, out):
    total = (mine[...] + other[...]).astype(BF)

    def step(d, _):
        out[d, :, 0:512] = dx[d]
        out[d, :, 512:896] = total
        return 0

    lax.fori_loop(0, 64, step, 0, unroll=8)


def spread(mine, other, dx):
    return pl.pallas_call(
        spread_kernel,
        out_shape=jax.ShapeDtypeStruct((64, 16, 896), BF),
        in_specs=[VM] * 3,
        out_specs=VM,
        compiler_params=pltpu.CompilerParams(vmem_limit_bytes=8 * MIB),
        name="spread_sums",
    )(mine, other, dx)


def finish_kernel(y, gain, wqkv, dx, qkv, proj, bias, ggain, weight, sem):
    copy = pltpu.make_async_copy(wqkv, weight, sem)
    copy.start()

    def step(s, _):
        dx[s, 0:16, :] = y[s, :, 0:256]
        dx[s, 16:32, :] = y[s, :, 256:512]
        return 0

    lax.fori_loop(0, 64, step, 0, unroll=8)
    for rb in range(16):
        rr = slice(16 * rb, 16 * rb + 16)
        qkv[rr, 0:384] = y[3 * rb, :, 512:896].astype(F32)
        qkv[rr, 384:768] = y[3 * rb + 1, :, 512:896].astype(F32)
        proj[rr, :] = y[3 * rb + 2, :, 512:768].astype(F32)
    for t in range(4):
        tile = [y[(t * 4 + r) * 3 + 2, :, 768:896].astype(F32) for r in range(4)]
        bias[128 * t : 128 * (t + 1), :] = jnp.concatenate(tile, 0).T
    copy.wait()
    along = jnp.sum(qkv[...] * weight[...].astype(F32), -1, keepdims=True)
    ggain[...] = jnp.broadcast_to(along, (256, 128)).T[0:1] / gain[...]


def finish(y, gain, wqkv):
    return pl.pallas_call(
        finish_kernel,
        out_shape=(
            jax.ShapeDtypeStruct((64, 32, 256), BF),
            jax.ShapeDtypeStruct((256, 768), F32),
            jax.ShapeDtypeStruct((256, 256), F32),
            jax.ShapeDtypeStruct((512, 64), F32),
            jax.ShapeDtypeStruct((1, 256), F32),
        ),
        in_specs=[VM, VM, HBM],
        out_specs=(VM,) * 5,
        scratch_shapes=[pltpu.VMEM((256, 768), BF), pltpu.SemaphoreType.DMA],
        compiler_params=pltpu.CompilerParams(vmem_limit_bytes=12 * MIB),
        name="place_results",
    )(y, gain, wqkv)


def on_device(activations, cotangent, ln_gain, qkv_weight, out_weight, position_bias):
    both = jnp.concatenate(
        [activations.reshape(64, 32, 256), cotangent.reshape(64, 32, 256)], axis=2
    )
    arrived = lax.all_to_all(both, CHIPS, 0, 0, tiled=True)
    gain = ln_gain.reshape(1, 256)
    partials, grad_packed = gradients(
        arrived, gain, qkv_weight, out_weight, position_bias.reshape(512, 64)
    )
    shares = lax.all_to_all(partials, CHIPS, 0, 0, tiled=True)
    message = input_gradient(arrived, grad_packed, gain, qkv_weight)
    shares, message = lax.optimization_barrier((shares, message))
    mine = jnp.sum(shares.astype(F32), axis=0)
    other = lax.ppermute(mine, "core", [(0, 1), (1, 0)])
    message = spread(mine, other, message)
    returned = lax.all_to_all(message, CHIPS, 0, 0, tiled=True)
    dx, grad_qkv, grad_proj, grad_bias, grad_gain = finish(returned, gain, qkv_weight)
    return (
        dx.reshape(activations.shape),
        grad_gain.reshape(256),
        grad_qkv,
        grad_proj,
        grad_bias.reshape(8, 64, 64),
    )


def solution(mesh):
    fine = jax.sharding.Mesh(mesh.devices.reshape(2, 4, 4, 2, 2), (*CHIPS, "core"))
    tokens = P(None, ("zl", "x"), ("y", "zh", "core"), None)
    return jax.shard_map(
        on_device,
        mesh=fine,
        in_specs=(tokens, tokens, P(), P(), P(), P()),
        out_specs=(tokens, P(), P(), P(), P()),
        check_vma=False,
    )
```

```python
import functools
import math

import jax
import jax.numpy as jnp
from jax import lax
from jax.experimental import pallas as pl
from jax.experimental.pallas import tpu as pltpu
from jax.sharding import PartitionSpec as P

F32 = jnp.float32
BF = jnp.bfloat16
MEMBERS = 64
GROUPS = 32
TOKENS = MEMBERS * GROUPS
SHARES = 64
SHARE = 36
HELD = 40
ROWS = SHARES * SHARE + HELD - SHARE
STRIDE = 40
SCALE = 32**-0.5
LOG2E = math.log2(math.e)
NN = (((1,), (0,)), ((), ()))
NT = (((1,), (1,)), ((), ()))
TN = (((0,), (0,)), ((), ()))
CHIPS = ("zl", "x", "y", "zh")
VM = pl.BlockSpec(memory_space=pltpu.VMEM)
HBM = pl.BlockSpec(memory_space=pltpu.HBM)
MIB = 2**20


def dot(a, b, dims):
    return lax.dot_general(a, b, dims, preferred_element_type=F32)


def unpack(recv, refs):
    def step(s, _):
        for i, ref in enumerate(refs):
            first, lane = GROUPS * (i // 2), 128 * (i % 2)
            rows = recv[s, first : first + GROUPS, lane : lane + 128]
            ref[pl.ds(s * STRIDE, GROUPS), :] = rows.astype(F32)
        return 0

    lax.fori_loop(0, MEMBERS, step, 0, unroll=8)


def grouped(refs, first, count):
    columns = [
        jnp.concatenate(
            [ref[pl.ds(first + k, MEMBERS, stride=STRIDE), :] for k in range(count)], axis=0
        )
        for ref in refs
    ]
    return jnp.concatenate(columns, axis=1)


def normalise(x):
    centred = x - jnp.mean(x, -1, keepdims=True)
    inverse = lax.rsqrt(jnp.mean(centred * centred, -1, keepdims=True) + 1e-5)
    return centred * inverse, inverse


def head_masks():
    lane = lax.broadcasted_iota(jnp.int32, (MEMBERS, 128), 1) // 32
    return [lane == h for h in range(4)]


def expand(a, masks):
    zero = jnp.zeros_like(a)
    return jnp.concatenate([jnp.where(m, a, zero) for m in masks], axis=0)


def pick(r, masks):
    out = r[0:MEMBERS]
    for h in range(1, 4):
        out = jnp.where(masks[h], r[MEMBERS * h : MEMBERS * (h + 1)], out)
    return out


def attention(count, q, k, v, da, bias, masks):
    units = [(g, hf) for g in range(count) for hf in range(2)]

    def part(a, u):
        g, hf = u
        return a[MEMBERS * g : MEMBERS * (g + 1), 128 * hf : 128 * (hf + 1)]

    qx = {u: expand(part(q, u), masks) for u in units}
    dax = {u: expand(part(da, u), masks) for u in units}
    scores = {}
    grad_probs = {}
    for u in units:
        scores[u] = dot(part(k, u), qx[u], NT)
        grad_probs[u] = dot(part(v, u), dax[u], NT)
    weights = {}
    scaled = {}
    grad_bias = [None, None]
    for u in units:
        hf = u[1]
        logits = scores[u] + bias[:, 256 * hf : 256 * (hf + 1)]
        e = jnp.exp2(logits - jnp.max(logits, 0, keepdims=True))
        p = e * (1.0 / jnp.sum(e, 0, keepdims=True))
        ds = p * (grad_probs[u] - jnp.sum(grad_probs[u] * p, 0, keepdims=True))
        weights[u] = p.astype(BF)
        scaled[u] = ds.astype(BF)
        grad_bias[hf] = ds if grad_bias[hf] is None else grad_bias[hf] + ds
    results = {}
    for u in units:
        attended = pick(dot(weights[u], part(v, u), TN), masks)
        grad_v = dot(weights[u], dax[u], NN)
        grad_k = dot(scaled[u], qx[u], NN) * (1.0 / LOG2E)
        grad_q = pick(dot(scaled[u], part(k, u), TN), masks) * SCALE
        results[u] = [r.astype(BF) for r in (attended, grad_q, grad_k, grad_v)]
    return results, grad_bias


def gradients_kernel(
    recv, gain, wqkv, wout, bias, msg, grad_packed,
    x0, x1, d0, d1, bias_t, grad_bias, normed_s, q_s, k_s, v_s, da_s, dy_s, att_s, gp_s, rows_s, sem,
):
    unpack(recv, (x0, x1, d0, d1))
    for t in range(4):
        bias_t[:, 128 * t : 128 * (t + 1)] = (bias[128 * t : 128 * (t + 1), :] * LOG2E).T
    grad_bias[...] = jnp.zeros_like(grad_bias)
    masks = head_masks()

    def project(b, _):
        rows = pl.ds(pl.multiple_of(b * 512, 512), 512)
        dy = grouped((d0, d1), b * 8, 8).astype(BF)
        dy_s[rows, :] = dy
        da_s[rows, :] = dot(dy, wout[...], NT).astype(BF)
        normal, _ = normalise(grouped((x0, x1), b * 8, 8))
        normed = (normal * gain[...]).astype(BF)
        normed_s[rows, :] = normed
        packed = dot(normed, wqkv[...], NN)
        q_s[rows, :] = (packed[:, :256] * (SCALE * LOG2E)).astype(BF)
        k_s[rows, :] = packed[:, 256:512].astype(BF)
        v_s[rows, :] = packed[:, 512:].astype(BF)
        return 0

    lax.fori_loop(0, GROUPS // 8, project, 0, unroll=4)

    def attend(b, _):
        rows = pl.ds(pl.multiple_of(b * 512, 512), 512)
        results, gb = attention(
            8, q_s[rows, :], k_s[rows, :], v_s[rows, :], da_s[rows, :], bias_t, masks
        )
        for (g, hf), (att, gq, gk, gv) in results.items():
            r = pl.ds(pl.multiple_of(b * 512 + MEMBERS * g, MEMBERS), MEMBERS)
            att_s[r, 128 * hf : 128 * (hf + 1)] = att
            for i, part in enumerate((gq, gk, gv)):
                gp_s[r, 256 * i + 128 * hf : 256 * i + 128 * (hf + 1)] = part
        for hf in range(2):
            grad_bias[:, 256 * hf : 256 * (hf + 1)] += gb[hf]
        return 0

    lax.fori_loop(0, GROUPS // 8, attend, 0, unroll=4)
    copy = pltpu.make_async_copy(gp_s, grad_packed, sem)
    copy.start()
    grad_qkv = dot(normed_s[...], gp_s[...], TN)
    grad_proj = dot(att_s[...], dy_s[...], TN)
    for t in range(6):
        rows_s[256 * t : 256 * (t + 1), :] = grad_qkv[:, 128 * t : 128 * (t + 1)]
    for t in range(2):
        rows_s[256 * (6 + t) : 256 * (7 + t), :] = grad_proj[:, 128 * t : 128 * (t + 1)]
    for t in range(4):
        rows_s[2048 + 64 * t : 2112 + 64 * t, :] = grad_bias[:, 128 * t : 128 * (t + 1)]
    rows_s[SHARES * SHARE :, :] = jnp.zeros((HELD - SHARE, 128), F32)
    for d in range(SHARES):
        msg[d] = rows_s[SHARE * d : SHARE * d + HELD, :].astype(BF)
    copy.wait()


def gradients(recv, gain, wqkv, wout, bias):
    return pl.pallas_call(
        gradients_kernel,
        out_shape=(
            jax.ShapeDtypeStruct((SHARES, HELD, 128), BF),
            jax.ShapeDtypeStruct((TOKENS, 768), BF),
        ),
        in_specs=[VM] * 5,
        out_specs=(VM, HBM),
        scratch_shapes=[
            *[pltpu.VMEM((MEMBERS * STRIDE, 128), F32)] * 4,
            *[pltpu.VMEM((MEMBERS, 512), F32)] * 2,
            *[pltpu.VMEM((TOKENS, 256), BF)] * 7,
            pltpu.VMEM((TOKENS, 768), BF),
            pltpu.VMEM((ROWS, 128), F32),
            pltpu.SemaphoreType.DMA,
        ],
        compiler_params=pltpu.CompilerParams(vmem_limit_bytes=50 * MIB),
        cost_estimate=pl.CostEstimate(
            flops=8 * 10**9, bytes_accessed=8 * 2**20, transcendentals=8 * 2**20
        ),
        name="parameter_gradients",
    )(recv, gain, wqkv, wout, bias)


def input_kernel(recv, grad_packed, gain, wqkv, out, x0, x1, d0, d1, gp_s, sem):
    copy = pltpu.make_async_copy(grad_packed, gp_s, sem)
    copy.start()
    unpack(recv, (x0, x1, d0, d1))
    copy.wait()

    def block(b, _):
        rows = pl.ds(pl.multiple_of(b * 512, 512), 512)
        g = dot(gp_s[rows, :], wqkv[...], NT) * gain[...]
        normal, inverse = normalise(grouped((x0, x1), b * 8, 8))
        along = jnp.mean(g * normal, -1, keepdims=True)
        dx = inverse * (g - jnp.mean(g, -1, keepdims=True) - normal * along)
        dx = grouped((d0, d1), b * 8, 8) + dx
        for k in range(8):
            for i, ref in enumerate((x0, x1)):
                ref[pl.ds(b * 8 + k, MEMBERS, stride=STRIDE), :] = dx[
                    MEMBERS * k : MEMBERS * (k + 1), 128 * i : 128 * (i + 1)
                ]
        return 0

    lax.fori_loop(0, GROUPS // 8, block, 0, unroll=4)

    def write(s, _):
        for i, ref in enumerate((x0, x1)):
            out[s, GROUPS * i : GROUPS * (i + 1), :] = ref[pl.ds(s * STRIDE, GROUPS), :].astype(BF)
        return 0

    lax.fori_loop(0, MEMBERS, write, 0, unroll=8)


def input_gradient(recv, grad_packed, gain, wqkv):
    return pl.pallas_call(
        input_kernel,
        out_shape=jax.ShapeDtypeStruct((MEMBERS, 2 * GROUPS, 128), BF),
        in_specs=[VM, HBM, VM, VM],
        out_specs=VM,
        scratch_shapes=[
            *[pltpu.VMEM((MEMBERS * STRIDE, 128), F32)] * 4,
            pltpu.VMEM((TOKENS, 768), BF),
            pltpu.SemaphoreType.DMA,
        ],
        compiler_params=pltpu.CompilerParams(vmem_limit_bytes=50 * MIB),
        cost_estimate=pl.CostEstimate(
            flops=6 * 10**9, bytes_accessed=16 * 2**20, transcendentals=2**20
        ),
        name="input_gradient",
    )(recv, grad_packed, gain, wqkv)


def spread_kernel(mine, other, dx, out):
    total = (mine[...] + other[...]).astype(BF)

    def step(d, _):
        out[d, 0:64, :] = dx[d]
        out[d, 64:, :] = total
        return 0

    lax.fori_loop(0, 64, step, 0, unroll=8)


def spread(mine, other, dx):
    return pl.pallas_call(
        spread_kernel,
        out_shape=jax.ShapeDtypeStruct((MEMBERS, 2 * GROUPS + HELD, 128), BF),
        in_specs=[VM] * 3,
        out_specs=VM,
        compiler_params=pltpu.CompilerParams(vmem_limit_bytes=8 * MIB),
        name="spread_sums",
    )(mine, other, dx)


def finish_kernel(y, gain, wqkv, dx, qkv, proj, bias, ggain, rows_s, weight, sem):
    copy = pltpu.make_async_copy(wqkv, weight, sem)
    copy.start()

    def step(s, _):
        dx[s, :, 0:128] = y[s, 0:32, :]
        dx[s, :, 128:256] = y[s, 32:64, :]
        return 0

    lax.fori_loop(0, 64, step, 0, unroll=8)
    for d in range(SHARES):
        rows_s[SHARE * d : SHARE * d + HELD, :] = y[d, 64:, :].astype(F32)
    for t in range(6):
        qkv[:, 128 * t : 128 * (t + 1)] = rows_s[256 * t : 256 * (t + 1), :]
    for t in range(2):
        proj[:, 128 * t : 128 * (t + 1)] = rows_s[256 * (6 + t) : 256 * (7 + t), :]
    for t in range(4):
        bias[128 * t : 128 * (t + 1), :] = rows_s[2048 + 64 * t : 2112 + 64 * t, :].T
    copy.wait()
    along = jnp.sum(qkv[...] * weight[...].astype(F32), -1, keepdims=True)
    ggain[...] = jnp.broadcast_to(along, (256, 128)).T[0:1] / gain[...]


def finish(y, gain, wqkv):
    return pl.pallas_call(
        finish_kernel,
        out_shape=(
            jax.ShapeDtypeStruct((64, 32, 256), BF),
            jax.ShapeDtypeStruct((256, 768), F32),
            jax.ShapeDtypeStruct((256, 256), F32),
            jax.ShapeDtypeStruct((512, 64), F32),
            jax.ShapeDtypeStruct((1, 256), F32),
        ),
        in_specs=[VM, VM, HBM],
        out_specs=(VM,) * 5,
        scratch_shapes=[
            pltpu.VMEM((ROWS, 128), F32),
            pltpu.VMEM((256, 768), BF),
            pltpu.SemaphoreType.DMA,
        ],
        compiler_params=pltpu.CompilerParams(vmem_limit_bytes=12 * MIB),
        name="place_results",
    )(y, gain, wqkv)


def on_device(activations, cotangent, ln_gain, qkv_weight, out_weight, position_bias):
    both = jnp.concatenate(
        [activations.reshape(64, 32, 256), cotangent.reshape(64, 32, 256)], axis=1
    )
    arrived = lax.all_to_all(both, CHIPS, 0, 0, tiled=True)
    gain = ln_gain.reshape(1, 256)
    partials, grad_packed = gradients(
        arrived, gain, qkv_weight, out_weight, position_bias.reshape(512, 64)
    )
    shares = lax.all_to_all(partials, CHIPS, 0, 0, tiled=True)
    message = input_gradient(arrived, grad_packed, gain, qkv_weight)
    shares, message = lax.optimization_barrier((shares, message))
    mine = jnp.sum(shares.astype(F32), axis=0)
    other = lax.ppermute(mine, "core", [(0, 1), (1, 0)])
    message = spread(mine, other, message)
    returned = lax.all_to_all(message, CHIPS, 0, 0, tiled=True)
    dx, grad_qkv, grad_proj, grad_bias, grad_gain = finish(returned, gain, qkv_weight)
    return (
        dx.reshape(activations.shape),
        grad_gain.reshape(256),
        grad_qkv,
        grad_proj,
        grad_bias.reshape(8, 64, 64),
    )


def solution(mesh):
    fine = jax.sharding.Mesh(mesh.devices.reshape(2, 4, 4, 2, 2), (*CHIPS, "core"))
    tokens = P(None, ("zl", "x"), ("y", "zh", "core"), None)
    return jax.shard_map(
        on_device,
        mesh=fine,
        in_specs=(tokens, tokens, P(), P(), P(), P()),
        out_specs=(tokens, P(), P(), P(), P()),
        check_vma=False,
    )
```

```python
import functools
import math

import jax
import jax.numpy as jnp
from jax import lax
from jax.experimental import pallas as pl
from jax.experimental.pallas import tpu as pltpu
from jax.sharding import PartitionSpec as P

F32 = jnp.float32
BF = jnp.bfloat16
MEMBERS = 64
GROUPS = 32
TOKENS = MEMBERS * GROUPS
SHARES = 64
SHARE = 36
HELD = 40
ROWS = SHARES * SHARE + HELD - SHARE
STRIDE = 40
SCALE = 32**-0.5
LOG2E = math.log2(math.e)
NN = (((1,), (0,)), ((), ()))
NT = (((1,), (1,)), ((), ()))
TN = (((0,), (0,)), ((), ()))
CHIPS = ("zl", "x", "y", "zh")
VM = pl.BlockSpec(memory_space=pltpu.VMEM)
HBM = pl.BlockSpec(memory_space=pltpu.HBM)
MIB = 2**20


def dot(a, b, dims):
    return lax.dot_general(a, b, dims, preferred_element_type=F32)


def unpack(recv, refs):
    def step(s, _):
        for i, ref in enumerate(refs):
            first, lane = GROUPS * (i // 2), 128 * (i % 2)
            rows = recv[s, first : first + GROUPS, lane : lane + 128]
            ref[pl.ds(s * STRIDE, GROUPS), :] = rows.astype(F32)
        return 0

    lax.fori_loop(0, MEMBERS, step, 0, unroll=8)


def grouped(refs, first, count):
    columns = [
        jnp.concatenate(
            [ref[pl.ds(first + k, MEMBERS, stride=STRIDE), :] for k in range(count)], axis=0
        )
        for ref in refs
    ]
    return jnp.concatenate(columns, axis=1)


def normalise(x):
    centred = x - jnp.mean(x, -1, keepdims=True)
    inverse = lax.rsqrt(jnp.mean(centred * centred, -1, keepdims=True) + 1e-5)
    return centred * inverse, inverse


def head_masks():
    lane = lax.broadcasted_iota(jnp.int32, (MEMBERS, 128), 1) // 32
    return [lane == h for h in range(4)]


def expand(a, masks):
    zero = jnp.zeros_like(a)
    return jnp.concatenate([jnp.where(m, a, zero) for m in masks], axis=0)


def pick(r, masks):
    out = r[0:MEMBERS]
    for h in range(1, 4):
        out = jnp.where(masks[h], r[MEMBERS * h : MEMBERS * (h + 1)], out)
    return out


def attention(count, q, k, v, da, bias, masks):
    units = [(g, hf) for g in range(count) for hf in range(2)]

    def part(a, u):
        g, hf = u
        return a[MEMBERS * g : MEMBERS * (g + 1), 128 * hf : 128 * (hf + 1)]

    def diagonal(a, b):
        zero = jnp.zeros_like(a)
        top = jnp.concatenate([a, zero], axis=1)
        return jnp.concatenate([top, jnp.concatenate([zero, b], axis=1)], axis=0)

    wide = {}
    products = {}
    for u in units:
        wide[u] = jnp.concatenate([expand(part(q, u), masks), expand(part(da, u), masks)], axis=1)
        products[u] = dot(diagonal(part(k, u), part(v, u)), wide[u], NT)
    stacked = {}
    grad_bias = [None, None]
    for u in units:
        hf = u[1]
        logits = products[u][:MEMBERS] + bias[:, 256 * hf : 256 * (hf + 1)]
        grad_probs = products[u][MEMBERS:]
        e = jnp.exp2(logits - jnp.max(logits, 0, keepdims=True))
        p = e * (1.0 / jnp.sum(e, 0, keepdims=True))
        ds = p * (grad_probs - jnp.sum(grad_probs * p, 0, keepdims=True))
        stacked[u] = jnp.concatenate([p.astype(BF), ds.astype(BF)], axis=0)
        grad_bias[hf] = ds if grad_bias[hf] is None else grad_bias[hf] + ds
    results = {}
    for u in units:
        down = dot(stacked[u], wide[u], NN)
        grad_v = down[:MEMBERS, 128:]
        grad_k = down[MEMBERS:, :128] * (1.0 / LOG2E)
        across = dot(stacked[u], diagonal(part(v, u), part(k, u)), TN)
        attended = pick(across[:, :128], masks)
        grad_q = pick(across[:, 128:], masks) * SCALE
        results[u] = [r.astype(BF) for r in (attended, grad_q, grad_k, grad_v)]
    return results, grad_bias


def gradients_kernel(
    recv, gain, wqkv, wout, bias, msg, grad_packed,
    x0, x1, d0, d1, bias_t, grad_bias, normed_s, q_s, k_s, v_s, da_s, dy_s, att_s, gp_s, rows_s, sem,
):
    unpack(recv, (x0, x1, d0, d1))
    for t in range(4):
        bias_t[:, 128 * t : 128 * (t + 1)] = (bias[128 * t : 128 * (t + 1), :] * LOG2E).T
    grad_bias[...] = jnp.zeros_like(grad_bias)
    masks = head_masks()

    def project(b, _):
        rows = pl.ds(pl.multiple_of(b * 512, 512), 512)
        dy = grouped((d0, d1), b * 8, 8).astype(BF)
        dy_s[rows, :] = dy
        da_s[rows, :] = dot(dy, wout[...], NT).astype(BF)
        normal, _ = normalise(grouped((x0, x1), b * 8, 8))
        normed = (normal * gain[...]).astype(BF)
        normed_s[rows, :] = normed
        packed = dot(normed, wqkv[...], NN)
        q_s[rows, :] = (packed[:, :256] * (SCALE * LOG2E)).astype(BF)
        k_s[rows, :] = packed[:, 256:512].astype(BF)
        v_s[rows, :] = packed[:, 512:].astype(BF)
        return 0

    lax.fori_loop(0, GROUPS // 8, project, 0, unroll=4)

    def keep(b):
        rows = pl.ds(pl.multiple_of(b * 512, 512), 512)
        return pltpu.make_async_copy(gp_s.at[rows, :], grad_packed.at[rows, :], sem.at[b])

    def attend(b, _):
        rows = pl.ds(pl.multiple_of(b * 512, 512), 512)
        results, gb = attention(
            8, q_s[rows, :], k_s[rows, :], v_s[rows, :], da_s[rows, :], bias_t, masks
        )
        for (g, hf), (att, gq, gk, gv) in results.items():
            r = pl.ds(pl.multiple_of(b * 512 + MEMBERS * g, MEMBERS), MEMBERS)
            att_s[r, 128 * hf : 128 * (hf + 1)] = att
            for i, part in enumerate((gq, gk, gv)):
                gp_s[r, 256 * i + 128 * hf : 256 * i + 128 * (hf + 1)] = part
        for hf in range(2):
            grad_bias[:, 256 * hf : 256 * (hf + 1)] += gb[hf]
        keep(b).start()
        return 0

    lax.fori_loop(0, GROUPS // 8, attend, 0, unroll=4)
    grad_qkv = dot(normed_s[...], gp_s[...], TN)
    grad_proj = dot(att_s[...], dy_s[...], TN)
    for t in range(6):
        rows_s[256 * t : 256 * (t + 1), :] = grad_qkv[:, 128 * t : 128 * (t + 1)]
    for t in range(2):
        rows_s[256 * (6 + t) : 256 * (7 + t), :] = grad_proj[:, 128 * t : 128 * (t + 1)]
    for t in range(4):
        rows_s[2048 + 64 * t : 2112 + 64 * t, :] = grad_bias[:, 128 * t : 128 * (t + 1)]
    rows_s[SHARES * SHARE :, :] = jnp.zeros((HELD - SHARE, 128), F32)
    for d in range(SHARES):
        msg[d] = rows_s[SHARE * d : SHARE * d + HELD, :].astype(BF)
    for b in range(GROUPS // 8):
        keep(b).wait()


def gradients(recv, gain, wqkv, wout, bias):
    return pl.pallas_call(
        gradients_kernel,
        out_shape=(
            jax.ShapeDtypeStruct((SHARES, HELD, 128), BF),
            jax.ShapeDtypeStruct((TOKENS, 768), BF),
        ),
        in_specs=[VM] * 5,
        out_specs=(VM, HBM),
        scratch_shapes=[
            *[pltpu.VMEM((MEMBERS * STRIDE, 128), F32)] * 4,
            *[pltpu.VMEM((MEMBERS, 512), F32)] * 2,
            *[pltpu.VMEM((TOKENS, 256), BF)] * 7,
            pltpu.VMEM((TOKENS, 768), BF),
            pltpu.VMEM((ROWS, 128), F32),
            pltpu.SemaphoreType.DMA((GROUPS // 8,)),
        ],
        compiler_params=pltpu.CompilerParams(vmem_limit_bytes=50 * MIB),
        cost_estimate=pl.CostEstimate(
            flops=8 * 10**9, bytes_accessed=8 * 2**20, transcendentals=8 * 2**20
        ),
        name="parameter_gradients",
    )(recv, gain, wqkv, wout, bias)


def input_kernel(recv, grad_packed, gain, wqkv, out, x0, x1, d0, d1, gp_s, sem):
    copy = pltpu.make_async_copy(grad_packed, gp_s, sem)
    copy.start()
    unpack(recv, (x0, x1, d0, d1))
    copy.wait()

    def block(b, _):
        rows = pl.ds(pl.multiple_of(b * 512, 512), 512)
        g = dot(gp_s[rows, :], wqkv[...], NT) * gain[...]
        normal, inverse = normalise(grouped((x0, x1), b * 8, 8))
        along = jnp.mean(g * normal, -1, keepdims=True)
        dx = inverse * (g - jnp.mean(g, -1, keepdims=True) - normal * along)
        dx = grouped((d0, d1), b * 8, 8) + dx
        for k in range(8):
            for i, ref in enumerate((x0, x1)):
                ref[pl.ds(b * 8 + k, MEMBERS, stride=STRIDE), :] = dx[
                    MEMBERS * k : MEMBERS * (k + 1), 128 * i : 128 * (i + 1)
                ]
        return 0

    lax.fori_loop(0, GROUPS // 8, block, 0, unroll=4)

    def write(s, _):
        for i, ref in enumerate((x0, x1)):
            out[s, GROUPS * i : GROUPS * (i + 1), :] = ref[pl.ds(s * STRIDE, GROUPS), :].astype(BF)
        return 0

    lax.fori_loop(0, MEMBERS, write, 0, unroll=8)


def input_gradient(recv, grad_packed, gain, wqkv):
    return pl.pallas_call(
        input_kernel,
        out_shape=jax.ShapeDtypeStruct((MEMBERS, 2 * GROUPS, 128), BF),
        in_specs=[VM, HBM, VM, VM],
        out_specs=VM,
        scratch_shapes=[
            *[pltpu.VMEM((MEMBERS * STRIDE, 128), F32)] * 4,
            pltpu.VMEM((TOKENS, 768), BF),
            pltpu.SemaphoreType.DMA,
        ],
        compiler_params=pltpu.CompilerParams(vmem_limit_bytes=50 * MIB),
        cost_estimate=pl.CostEstimate(
            flops=6 * 10**9, bytes_accessed=16 * 2**20, transcendentals=2**20
        ),
        name="input_gradient",
    )(recv, grad_packed, gain, wqkv)


def spread_kernel(mine, other, dx, out):
    total = (mine[...] + other[...]).astype(BF)

    def step(d, _):
        out[d, 0:64, :] = dx[d]
        out[d, 64:, :] = total
        return 0

    lax.fori_loop(0, 64, step, 0, unroll=8)


def spread(mine, other, dx):
    return pl.pallas_call(
        spread_kernel,
        out_shape=jax.ShapeDtypeStruct((MEMBERS, 2 * GROUPS + HELD, 128), BF),
        in_specs=[VM] * 3,
        out_specs=VM,
        compiler_params=pltpu.CompilerParams(vmem_limit_bytes=8 * MIB),
        name="spread_sums",
    )(mine, other, dx)


def finish_kernel(y, gain, wqkv, dx, qkv, proj, bias, ggain, rows_s, weight, sem):
    copy = pltpu.make_async_copy(wqkv, weight, sem)
    copy.start()

    def step(s, _):
        dx[s, :, 0:128] = y[s, 0:32, :]
        dx[s, :, 128:256] = y[s, 32:64, :]
        return 0

    lax.fori_loop(0, 64, step, 0, unroll=8)
    for d in range(SHARES):
        rows_s[SHARE * d : SHARE * d + HELD, :] = y[d, 64:, :].astype(F32)
    for t in range(6):
        qkv[:, 128 * t : 128 * (t + 1)] = rows_s[256 * t : 256 * (t + 1), :]
    for t in range(2):
        proj[:, 128 * t : 128 * (t + 1)] = rows_s[256 * (6 + t) : 256 * (7 + t), :]
    for t in range(4):
        bias[128 * t : 128 * (t + 1), :] = rows_s[2048 + 64 * t : 2112 + 64 * t, :].T
    copy.wait()
    along = jnp.sum(qkv[...] * weight[...].astype(F32), -1, keepdims=True)
    ggain[...] = jnp.broadcast_to(along, (256, 128)).T[0:1] / gain[...]


def finish(y, gain, wqkv):
    return pl.pallas_call(
        finish_kernel,
        out_shape=(
            jax.ShapeDtypeStruct((64, 32, 256), BF),
            jax.ShapeDtypeStruct((256, 768), F32),
            jax.ShapeDtypeStruct((256, 256), F32),
            jax.ShapeDtypeStruct((512, 64), F32),
            jax.ShapeDtypeStruct((1, 256), F32),
        ),
        in_specs=[VM, VM, HBM],
        out_specs=(VM,) * 5,
        scratch_shapes=[
            pltpu.VMEM((ROWS, 128), F32),
            pltpu.VMEM((256, 768), BF),
            pltpu.SemaphoreType.DMA,
        ],
        compiler_params=pltpu.CompilerParams(vmem_limit_bytes=12 * MIB),
        name="place_results",
    )(y, gain, wqkv)


def on_device(activations, cotangent, ln_gain, qkv_weight, out_weight, position_bias):
    both = jnp.concatenate(
        [activations.reshape(64, 32, 256), cotangent.reshape(64, 32, 256)], axis=1
    )
    arrived = lax.all_to_all(both, CHIPS, 0, 0, tiled=True)
    gain = ln_gain.reshape(1, 256)
    partials, grad_packed = gradients(
        arrived, gain, qkv_weight, out_weight, position_bias.reshape(512, 64)
    )
    shares = lax.all_to_all(partials, CHIPS, 0, 0, tiled=True)
    message = input_gradient(arrived, grad_packed, gain, qkv_weight)
    shares, message = lax.optimization_barrier((shares, message))
    mine = jnp.sum(shares.astype(F32), axis=0)
    other = lax.ppermute(mine, "core", [(0, 1), (1, 0)])
    message = spread(mine, other, message)
    returned = lax.all_to_all(message, CHIPS, 0, 0, tiled=True)
    dx, grad_qkv, grad_proj, grad_bias, grad_gain = finish(returned, gain, qkv_weight)
    return (
        dx.reshape(activations.shape),
        grad_gain.reshape(256),
        grad_qkv,
        grad_proj,
        grad_bias.reshape(8, 64, 64),
    )


def solution(mesh):
    fine = jax.sharding.Mesh(mesh.devices.reshape(2, 4, 4, 2, 2), (*CHIPS, "core"))
    tokens = P(None, ("zl", "x"), ("y", "zh", "core"), None)
    return jax.shard_map(
        on_device,
        mesh=fine,
        in_specs=(tokens, tokens, P(), P(), P(), P()),
        out_specs=(tokens, P(), P(), P(), P()),
        check_vma=False,
    )
```

```python
import functools
import math

import jax
import jax.numpy as jnp
from jax import lax
from jax.experimental import pallas as pl
from jax.experimental.pallas import tpu as pltpu
from jax.sharding import PartitionSpec as P

F32 = jnp.float32
BF = jnp.bfloat16
MEMBERS = 64
GROUPS = 32
TOKENS = MEMBERS * GROUPS
SHARES = 64
SHARE = 36
HELD = 40
ROWS = SHARES * SHARE + HELD - SHARE
STRIDE = 40
SCALE = 32**-0.5
LOG2E = math.log2(math.e)
NN = (((1,), (0,)), ((), ()))
NT = (((1,), (1,)), ((), ()))
TN = (((0,), (0,)), ((), ()))
CHIPS = ("zl", "x", "y", "zh")
VM = pl.BlockSpec(memory_space=pltpu.VMEM)
HBM = pl.BlockSpec(memory_space=pltpu.HBM)
MIB = 2**20


def dot(a, b, dims):
    return lax.dot_general(a, b, dims, preferred_element_type=F32)


def unpack(recv, refs):
    def step(s, _):
        for i, ref in enumerate(refs):
            first, lane = GROUPS * (i // 2), 128 * (i % 2)
            rows = recv[s, first : first + GROUPS, lane : lane + 128]
            ref[pl.ds(s * STRIDE, GROUPS), :] = rows.astype(F32)
        return 0

    lax.fori_loop(0, MEMBERS, step, 0, unroll=8)


def grouped(refs, first, count):
    columns = [
        jnp.concatenate(
            [ref[pl.ds(first + k, MEMBERS, stride=STRIDE), :] for k in range(count)], axis=0
        )
        for ref in refs
    ]
    return jnp.concatenate(columns, axis=1)


def normalise(x):
    centred = x - jnp.mean(x, -1, keepdims=True)
    inverse = lax.rsqrt(jnp.mean(centred * centred, -1, keepdims=True) + 1e-5)
    return centred * inverse, inverse


def head_masks():
    lane = lax.broadcasted_iota(jnp.int32, (MEMBERS, 128), 1) // 32
    return [lane == h for h in range(4)]


def expand(a, masks):
    zero = jnp.zeros_like(a)
    return jnp.concatenate([jnp.where(m, a, zero) for m in masks], axis=0)


def pick(r, masks):
    out = r[0:MEMBERS]
    for h in range(1, 4):
        out = jnp.where(masks[h], r[MEMBERS * h : MEMBERS * (h + 1)], out)
    return out


def attention(count, q, k, v, da, bias, masks):
    units = [(g, hf) for g in range(count) for hf in range(2)]

    def part(a, u):
        g, hf = u
        return a[MEMBERS * g : MEMBERS * (g + 1), 128 * hf : 128 * (hf + 1)]

    def diagonal(a, b):
        zero = jnp.zeros_like(a)
        top = jnp.concatenate([a, zero], axis=1)
        return jnp.concatenate([top, jnp.concatenate([zero, b], axis=1)], axis=0)

    wide = {}
    products = {}
    for u in units:
        wide[u] = jnp.concatenate([expand(part(q, u), masks), expand(part(da, u), masks)], axis=1)
        products[u] = dot(diagonal(part(k, u), part(v, u)), wide[u], NT)
    stacked = {}
    grad_bias = [None, None]
    for u in units:
        hf = u[1]
        logits = products[u][:MEMBERS] + bias[:, 256 * hf : 256 * (hf + 1)]
        grad_probs = products[u][MEMBERS:]
        e = jnp.exp2(logits - jnp.max(logits, 0, keepdims=True))
        p = e * (1.0 / jnp.sum(e, 0, keepdims=True))
        ds = p * (grad_probs - jnp.sum(grad_probs * p, 0, keepdims=True))
        stacked[u] = jnp.concatenate([p.astype(BF), ds.astype(BF)], axis=0)
        grad_bias[hf] = ds if grad_bias[hf] is None else grad_bias[hf] + ds
    results = {}
    for u in units:
        down = dot(stacked[u], wide[u], NN)
        grad_v = down[:MEMBERS, 128:]
        grad_k = down[MEMBERS:, :128] * (1.0 / LOG2E)
        across = dot(stacked[u], diagonal(part(v, u), part(k, u)), TN)
        attended = pick(across[:, :128], masks)
        grad_q = pick(across[:, 128:], masks) * SCALE
        results[u] = [r.astype(BF) for r in (attended, grad_q, grad_k, grad_v)]
    return results, grad_bias


def gradients_kernel(
    recv, gain, wqkv, wout, bias, msg, x0, x1, d0, d1, bias_t, grad_bias,
    normal_s, inverse_s, normed_s, q_s, k_s, v_s, da_s, dy_s, att_s, gp_s, rows_s,
):
    unpack(recv, (x0, x1, d0, d1))
    for t in range(4):
        bias_t[:, 128 * t : 128 * (t + 1)] = (bias[128 * t : 128 * (t + 1), :] * LOG2E).T
    grad_bias[...] = jnp.zeros_like(grad_bias)
    masks = head_masks()

    def project(b, _):
        rows = pl.ds(pl.multiple_of(b * 512, 512), 512)
        dy = grouped((d0, d1), b * 8, 8).astype(BF)
        dy_s[rows, :] = dy
        da_s[rows, :] = dot(dy, wout[...], NT).astype(BF)
        normal, inverse = normalise(grouped((x0, x1), b * 8, 8))
        normal_s[rows, :] = normal
        inverse_s[rows, :] = jnp.broadcast_to(inverse, (512, 128))
        normed = (normal * gain[...]).astype(BF)
        normed_s[rows, :] = normed
        packed = dot(normed, wqkv[...], NN)
        q_s[rows, :] = (packed[:, :256] * (SCALE * LOG2E)).astype(BF)
        k_s[rows, :] = packed[:, 256:512].astype(BF)
        v_s[rows, :] = packed[:, 512:].astype(BF)
        return 0

    lax.fori_loop(0, GROUPS // 8, project, 0, unroll=4)

    def attend(b, _):
        rows = pl.ds(pl.multiple_of(b * 512, 512), 512)
        results, gb = attention(
            8, q_s[rows, :], k_s[rows, :], v_s[rows, :], da_s[rows, :], bias_t, masks
        )
        for (g, hf), (att, gq, gk, gv) in results.items():
            r = pl.ds(pl.multiple_of(b * 512 + MEMBERS * g, MEMBERS), MEMBERS)
            att_s[r, 128 * hf : 128 * (hf + 1)] = att
            for i, part in enumerate((gq, gk, gv)):
                gp_s[r, 256 * i + 128 * hf : 256 * i + 128 * (hf + 1)] = part
        for hf in range(2):
            grad_bias[:, 256 * hf : 256 * (hf + 1)] += gb[hf]
        return 0

    lax.fori_loop(0, GROUPS // 8, attend, 0, unroll=4)
    grad_qkv = dot(normed_s[...], gp_s[...], TN)
    grad_proj = dot(att_s[...], dy_s[...], TN)
    for t in range(6):
        rows_s[256 * t : 256 * (t + 1), :] = grad_qkv[:, 128 * t : 128 * (t + 1)]
    for t in range(2):
        rows_s[256 * (6 + t) : 256 * (7 + t), :] = grad_proj[:, 128 * t : 128 * (t + 1)]
    for t in range(4):
        rows_s[2048 + 64 * t : 2112 + 64 * t, :] = grad_bias[:, 128 * t : 128 * (t + 1)]
    rows_s[SHARES * SHARE :, :] = jnp.zeros((HELD - SHARE, 128), F32)
    for d in range(SHARES):
        msg[d, 2 * GROUPS :, :] = rows_s[SHARE * d : SHARE * d + HELD, :].astype(BF)

    def pull_back(b, _):
        rows = pl.ds(pl.multiple_of(b * 512, 512), 512)
        g = dot(gp_s[rows, :], wqkv[...], NT) * gain[...]
        normal = normal_s[rows, :]
        inverse = jnp.concatenate([inverse_s[rows, :]] * 2, axis=1)
        along = jnp.mean(g * normal, -1, keepdims=True)
        dx = inverse * (g - jnp.mean(g, -1, keepdims=True) - normal * along)
        dx = dy_s[rows, :].astype(F32) + dx
        for k in range(8):
            for i, ref in enumerate((x0, x1)):
                ref[pl.ds(b * 8 + k, MEMBERS, stride=STRIDE), :] = dx[
                    MEMBERS * k : MEMBERS * (k + 1), 128 * i : 128 * (i + 1)
                ]
        return 0

    lax.fori_loop(0, GROUPS // 8, pull_back, 0, unroll=4)

    def write(s, _):
        for i, ref in enumerate((x0, x1)):
            msg[s, GROUPS * i : GROUPS * (i + 1), :] = ref[pl.ds(s * STRIDE, GROUPS), :].astype(BF)
        return 0

    lax.fori_loop(0, MEMBERS, write, 0, unroll=8)


def gradients(recv, gain, wqkv, wout, bias):
    return pl.pallas_call(
        gradients_kernel,
        out_shape=jax.ShapeDtypeStruct((MEMBERS, 2 * GROUPS + HELD, 128), BF),
        in_specs=[VM] * 5,
        out_specs=VM,
        scratch_shapes=[
            *[pltpu.VMEM((MEMBERS * STRIDE, 128), F32)] * 4,
            *[pltpu.VMEM((MEMBERS, 512), F32)] * 2,
            pltpu.VMEM((TOKENS, 256), F32),
            pltpu.VMEM((TOKENS, 128), F32),
            *[pltpu.VMEM((TOKENS, 256), BF)] * 7,
            pltpu.VMEM((TOKENS, 768), BF),
            pltpu.VMEM((ROWS, 128), F32),
        ],
        compiler_params=pltpu.CompilerParams(vmem_limit_bytes=40 * MIB),
        name="layer_gradients",
    )(recv, gain, wqkv, wout, bias)


def finish_kernel(y, sums, gain, wqkv, dx, qkv, proj, bias, ggain, rows_s, weight, sem):
    copy = pltpu.make_async_copy(wqkv, weight, sem)
    copy.start()

    def step(s, _):
        dx[s, :, 0:128] = y[s, 0:32, :]
        dx[s, :, 128:256] = y[s, 32:64, :]
        return 0

    lax.fori_loop(0, 64, step, 0, unroll=8)
    for d in range(SHARES):
        share = sums[d].astype(F32)
        row = SHARE * d
        while row < SHARE * (d + 1):
            t, r = divmod(row, 256)
            count = min(256 - r, SHARE * (d + 1) - row)
            part = share[row - SHARE * d : row - SHARE * d + count]
            if t < 6:
                qkv[r : r + count, 128 * t : 128 * (t + 1)] = part
            elif t < 8:
                proj[r : r + count, 128 * (t - 6) : 128 * (t - 5)] = part
            else:
                rows_s[r : r + count, :] = part
            row += count
    for t in range(4):
        bias[128 * t : 128 * (t + 1), :] = rows_s[64 * t : 64 * (t + 1), :].T
    copy.wait()
    along = jnp.sum(qkv[...] * weight[...].astype(F32), -1, keepdims=True)
    ggain[...] = jnp.broadcast_to(along, (256, 128)).T[0:1] / gain[...]


def finish(y, sums, gain, wqkv):
    return pl.pallas_call(
        finish_kernel,
        out_shape=(
            jax.ShapeDtypeStruct((64, 32, 256), BF),
            jax.ShapeDtypeStruct((256, 768), F32),
            jax.ShapeDtypeStruct((256, 256), F32),
            jax.ShapeDtypeStruct((512, 64), F32),
            jax.ShapeDtypeStruct((1, 256), F32),
        ),
        in_specs=[VM, VM, VM, HBM],
        out_specs=(VM,) * 5,
        scratch_shapes=[
            pltpu.VMEM((256, 128), F32),
            pltpu.VMEM((256, 768), BF),
            pltpu.SemaphoreType.DMA,
        ],
        compiler_params=pltpu.CompilerParams(vmem_limit_bytes=12 * MIB),
        name="place_results",
    )(y, sums, gain, wqkv)


def on_device(activations, cotangent, ln_gain, qkv_weight, out_weight, position_bias):
    both = jnp.concatenate(
        [activations.reshape(64, 32, 256), cotangent.reshape(64, 32, 256)], axis=1
    )
    arrived = lax.all_to_all(both, CHIPS, 0, 0, tiled=True)
    gain = ln_gain.reshape(1, 256)
    message = gradients(arrived, gain, qkv_weight, out_weight, position_bias.reshape(512, 64))
    returned = lax.all_to_all(message, CHIPS, 0, 0, tiled=True)
    mine = jnp.sum(returned[:, 2 * GROUPS :, :].astype(F32), axis=0)
    other = lax.ppermute(mine, "core", [(0, 1), (1, 0)])
    total = jnp.broadcast_to((mine + other).astype(BF), (SHARES, HELD, 128))
    sums = lax.all_to_all(total, CHIPS, 0, 0, tiled=True)
    dx, grad_qkv, grad_proj, grad_bias, grad_gain = finish(returned, sums, gain, qkv_weight)
    return (
        dx.reshape(activations.shape),
        grad_gain.reshape(256),
        grad_qkv,
        grad_proj,
        grad_bias.reshape(8, 64, 64),
    )


def solution(mesh):
    fine = jax.sharding.Mesh(mesh.devices.reshape(2, 4, 4, 2, 2), (*CHIPS, "core"))
    tokens = P(None, ("zl", "x"), ("y", "zh", "core"), None)
    return jax.shard_map(
        on_device,
        mesh=fine,
        in_specs=(tokens, tokens, P(), P(), P(), P()),
        out_specs=(tokens, P(), P(), P(), P()),
        check_vma=False,
    )
```

```python
import functools
import math

import jax
import jax.numpy as jnp
from jax import lax
from jax.experimental import pallas as pl
from jax.experimental.pallas import tpu as pltpu
from jax.sharding import PartitionSpec as P

F32 = jnp.float32
BF = jnp.bfloat16
MEMBERS = 64
GROUPS = 32
TOKENS = MEMBERS * GROUPS
SHARES = 64
SHARE = 36
HELD = 40
ROWS = SHARES * SHARE + HELD - SHARE
STRIDE = 40
SCALE = 32**-0.5
LOG2E = math.log2(math.e)
NN = (((1,), (0,)), ((), ()))
NT = (((1,), (1,)), ((), ()))
TN = (((0,), (0,)), ((), ()))
CHIPS = ("zl", "x", "y", "zh")
VM = pl.BlockSpec(memory_space=pltpu.VMEM)
HBM = pl.BlockSpec(memory_space=pltpu.HBM)
MIB = 2**20


def dot(a, b, dims):
    return lax.dot_general(a, b, dims, preferred_element_type=F32)


def unpack(recv, refs):
    def step(s, _):
        for i, ref in enumerate(refs):
            first, lane = GROUPS * (i // 2), 128 * (i % 2)
            rows = recv[s, first : first + GROUPS, lane : lane + 128]
            ref[pl.ds(s * STRIDE, GROUPS), :] = rows.astype(F32)
        return 0

    lax.fori_loop(0, MEMBERS, step, 0, unroll=8)


def grouped(refs, first, count):
    columns = [
        jnp.concatenate(
            [ref[pl.ds(first + k, MEMBERS, stride=STRIDE), :] for k in range(count)], axis=0
        )
        for ref in refs
    ]
    return jnp.concatenate(columns, axis=1)


def normalise(x):
    centred = x - jnp.mean(x, -1, keepdims=True)
    inverse = lax.rsqrt(jnp.mean(centred * centred, -1, keepdims=True) + 1e-5)
    return centred * inverse, inverse


def head_masks():
    lane = lax.broadcasted_iota(jnp.int32, (MEMBERS, 128), 1) // 32
    return [lane == h for h in range(4)]


def expand(a, masks):
    zero = jnp.zeros_like(a)
    return jnp.concatenate([jnp.where(m, a, zero) for m in masks], axis=0)


def pick(r, masks):
    out = r[0:MEMBERS]
    for h in range(1, 4):
        out = jnp.where(masks[h], r[MEMBERS * h : MEMBERS * (h + 1)], out)
    return out


def attention(count, q, k, v, da, bias, masks):
    units = [(g, hf) for g in range(count) for hf in range(2)]

    def part(a, u):
        g, hf = u
        return a[MEMBERS * g : MEMBERS * (g + 1), 128 * hf : 128 * (hf + 1)]

    def diagonal(a, b):
        zero = jnp.zeros_like(a)
        top = jnp.concatenate([a, zero], axis=1)
        return jnp.concatenate([top, jnp.concatenate([zero, b], axis=1)], axis=0)

    wide = {}
    products = {}
    for u in units:
        wide[u] = jnp.concatenate([expand(part(q, u), masks), expand(part(da, u), masks)], axis=1)
        products[u] = dot(diagonal(part(k, u), part(v, u)), wide[u], NT)
    stacked = {}
    grad_bias = [None, None]
    for u in units:
        hf = u[1]
        logits = products[u][:MEMBERS] + bias[:, 256 * hf : 256 * (hf + 1)]
        grad_probs = products[u][MEMBERS:]
        e = jnp.exp2(logits - jnp.max(logits, 0, keepdims=True))
        p = e * (1.0 / jnp.sum(e, 0, keepdims=True))
        ds = p * (grad_probs - jnp.sum(grad_probs * p, 0, keepdims=True))
        stacked[u] = jnp.concatenate([p.astype(BF), ds.astype(BF)], axis=0)
        grad_bias[hf] = ds if grad_bias[hf] is None else grad_bias[hf] + ds
    results = {}
    for u in units:
        down = dot(stacked[u], wide[u], NN)
        grad_v = down[:MEMBERS, 128:]
        grad_k = down[MEMBERS:, :128] * (1.0 / LOG2E)
        across = dot(stacked[u], diagonal(part(v, u), part(k, u)), TN)
        attended = pick(across[:, :128], masks)
        grad_q = pick(across[:, 128:], masks) * SCALE
        results[u] = [r.astype(BF) for r in (attended, grad_q, grad_k, grad_v)]
    return results, grad_bias


def gradients_kernel(
    recv, gain, wqkv, wout, bias, msg, x0, x1, d0, d1, bias_t, grad_bias,
    normal_s, inverse_s, normed_s, q_s, k_s, v_s, da_s, dy_s, att_s, gp_s, rows_s,
):
    unpack(recv, (x0, x1, d0, d1))
    for t in range(4):
        bias_t[:, 128 * t : 128 * (t + 1)] = (bias[128 * t : 128 * (t + 1), :] * LOG2E).T
    grad_bias[...] = jnp.zeros_like(grad_bias)
    masks = head_masks()

    def project(b, _):
        rows = pl.ds(pl.multiple_of(b * 512, 512), 512)
        dy = grouped((d0, d1), b * 8, 8).astype(BF)
        dy_s[rows, :] = dy
        da_s[rows, :] = dot(dy, wout[...], NT).astype(BF)
        normal, inverse = normalise(grouped((x0, x1), b * 8, 8))
        normal_s[rows, :] = normal
        inverse_s[rows, :] = jnp.broadcast_to(inverse, (512, 128))
        normed = (normal * gain[...]).astype(BF)
        normed_s[rows, :] = normed
        packed = dot(normed, wqkv[...], NN)
        q_s[rows, :] = (packed[:, :256] * (SCALE * LOG2E)).astype(BF)
        k_s[rows, :] = packed[:, 256:512].astype(BF)
        v_s[rows, :] = packed[:, 512:].astype(BF)
        return 0

    lax.fori_loop(0, GROUPS // 8, project, 0, unroll=4)

    def attend(b, _):
        rows = pl.ds(pl.multiple_of(b * 512, 512), 512)
        results, gb = attention(
            8, q_s[rows, :], k_s[rows, :], v_s[rows, :], da_s[rows, :], bias_t, masks
        )
        for (g, hf), (att, gq, gk, gv) in results.items():
            r = pl.ds(pl.multiple_of(b * 512 + MEMBERS * g, MEMBERS), MEMBERS)
            att_s[r, 128 * hf : 128 * (hf + 1)] = att
            for i, part in enumerate((gq, gk, gv)):
                gp_s[r, 256 * i + 128 * hf : 256 * i + 128 * (hf + 1)] = part
        for hf in range(2):
            grad_bias[:, 256 * hf : 256 * (hf + 1)] += gb[hf]
        return 0

    lax.fori_loop(0, GROUPS // 8, attend, 0, unroll=4)
    def pull_back(b, _):
        rows = pl.ds(pl.multiple_of(b * 512, 512), 512)
        g = dot(gp_s[rows, :], wqkv[...], NT) * gain[...]
        normal = normal_s[rows, :]
        inverse = jnp.concatenate([inverse_s[rows, :]] * 2, axis=1)
        along = jnp.mean(g * normal, -1, keepdims=True)
        dx = inverse * (g - jnp.mean(g, -1, keepdims=True) - normal * along)
        dx = dy_s[rows, :].astype(F32) + dx
        for k in range(8):
            for i, ref in enumerate((x0, x1)):
                ref[pl.ds(b * 8 + k, MEMBERS, stride=STRIDE), :] = dx[
                    MEMBERS * k : MEMBERS * (k + 1), 128 * i : 128 * (i + 1)
                ]
        return 0

    lax.fori_loop(0, GROUPS // 8, pull_back, 0, unroll=4)

    grad_qkv = dot(normed_s[...], gp_s[...], TN)
    grad_proj = dot(att_s[...], dy_s[...], TN)
    for t in range(6):
        rows_s[256 * t : 256 * (t + 1), :] = grad_qkv[:, 128 * t : 128 * (t + 1)]
    for t in range(2):
        rows_s[256 * (6 + t) : 256 * (7 + t), :] = grad_proj[:, 128 * t : 128 * (t + 1)]
    for t in range(4):
        rows_s[2048 + 64 * t : 2112 + 64 * t, :] = grad_bias[:, 128 * t : 128 * (t + 1)]
    rows_s[SHARES * SHARE :, :] = jnp.zeros((HELD - SHARE, 128), F32)
    for d in range(SHARES):
        msg[d, 2 * GROUPS :, :] = rows_s[SHARE * d : SHARE * d + HELD, :].astype(BF)

    def write(s, _):
        for i, ref in enumerate((x0, x1)):
            msg[s, GROUPS * i : GROUPS * (i + 1), :] = ref[pl.ds(s * STRIDE, GROUPS), :].astype(BF)
        return 0

    lax.fori_loop(0, MEMBERS, write, 0, unroll=8)


def gradients(recv, gain, wqkv, wout, bias):
    return pl.pallas_call(
        gradients_kernel,
        out_shape=jax.ShapeDtypeStruct((MEMBERS, 2 * GROUPS + HELD, 128), BF),
        in_specs=[VM] * 5,
        out_specs=VM,
        scratch_shapes=[
            *[pltpu.VMEM((MEMBERS * STRIDE, 128), F32)] * 4,
            *[pltpu.VMEM((MEMBERS, 512), F32)] * 2,
            pltpu.VMEM((TOKENS, 256), F32),
            pltpu.VMEM((TOKENS, 128), F32),
            *[pltpu.VMEM((TOKENS, 256), BF)] * 7,
            pltpu.VMEM((TOKENS, 768), BF),
            pltpu.VMEM((ROWS, 128), F32),
        ],
        compiler_params=pltpu.CompilerParams(vmem_limit_bytes=40 * MIB),
        name="layer_gradients",
    )(recv, gain, wqkv, wout, bias)


def finish_kernel(y, sums, gain, wqkv, dx, qkv, proj, bias, ggain, rows_s, weight, sem):
    copy = pltpu.make_async_copy(wqkv, weight, sem)
    copy.start()

    def step(s, _):
        dx[s, :, 0:128] = y[s, 0:32, :]
        dx[s, :, 128:256] = y[s, 32:64, :]
        return 0

    lax.fori_loop(0, 64, step, 0, unroll=8)
    for d in range(SHARES):
        share = sums[d].astype(F32)
        row = SHARE * d
        while row < SHARE * (d + 1):
            t, r = divmod(row, 256)
            count = min(256 - r, SHARE * (d + 1) - row)
            part = share[row - SHARE * d : row - SHARE * d + count]
            if t < 6:
                qkv[r : r + count, 128 * t : 128 * (t + 1)] = part
            elif t < 8:
                proj[r : r + count, 128 * (t - 6) : 128 * (t - 5)] = part
            else:
                rows_s[r : r + count, :] = part
            row += count
    for t in range(4):
        bias[128 * t : 128 * (t + 1), :] = rows_s[64 * t : 64 * (t + 1), :].T
    copy.wait()
    along = jnp.sum(qkv[...] * weight[...].astype(F32), -1, keepdims=True)
    ggain[...] = jnp.broadcast_to(along, (256, 128)).T[0:1] / gain[...]


def finish(y, sums, gain, wqkv):
    return pl.pallas_call(
        finish_kernel,
        out_shape=(
            jax.ShapeDtypeStruct((64, 32, 256), BF),
            jax.ShapeDtypeStruct((256, 768), F32),
            jax.ShapeDtypeStruct((256, 256), F32),
            jax.ShapeDtypeStruct((512, 64), F32),
            jax.ShapeDtypeStruct((1, 256), F32),
        ),
        in_specs=[VM, VM, VM, HBM],
        out_specs=(VM,) * 5,
        scratch_shapes=[
            pltpu.VMEM((256, 128), F32),
            pltpu.VMEM((256, 768), BF),
            pltpu.SemaphoreType.DMA,
        ],
        compiler_params=pltpu.CompilerParams(vmem_limit_bytes=12 * MIB),
        name="place_results",
    )(y, sums, gain, wqkv)


def on_device(activations, cotangent, ln_gain, qkv_weight, out_weight, position_bias):
    both = jnp.concatenate(
        [activations.reshape(64, 32, 256), cotangent.reshape(64, 32, 256)], axis=1
    )
    arrived = lax.all_to_all(both, CHIPS, 0, 0, tiled=True)
    gain = ln_gain.reshape(1, 256)
    message = gradients(arrived, gain, qkv_weight, out_weight, position_bias.reshape(512, 64))
    returned = lax.all_to_all(message, CHIPS, 0, 0, tiled=True)
    mine = jnp.sum(returned[:, 2 * GROUPS :, :].astype(F32), axis=0)
    other = lax.ppermute(mine, "core", [(0, 1), (1, 0)])
    total = jnp.broadcast_to((mine + other).astype(BF), (SHARES, HELD, 128))
    sums = lax.all_to_all(total, CHIPS, 0, 0, tiled=True)
    dx, grad_qkv, grad_proj, grad_bias, grad_gain = finish(returned, sums, gain, qkv_weight)
    return (
        dx.reshape(activations.shape),
        grad_gain.reshape(256),
        grad_qkv,
        grad_proj,
        grad_bias.reshape(8, 64, 64),
    )


def solution(mesh):
    fine = jax.sharding.Mesh(mesh.devices.reshape(2, 4, 4, 2, 2), (*CHIPS, "core"))
    tokens = P(None, ("zl", "x"), ("y", "zh", "core"), None)
    return jax.shard_map(
        on_device,
        mesh=fine,
        in_specs=(tokens, tokens, P(), P(), P(), P()),
        out_specs=(tokens, P(), P(), P(), P()),
        check_vma=False,
    )
```

```python
import functools
import math

import jax
import jax.numpy as jnp
from jax import lax
from jax.experimental import pallas as pl
from jax.experimental.pallas import tpu as pltpu
from jax.sharding import PartitionSpec as P

F32 = jnp.float32
BF = jnp.bfloat16
MEMBERS = 64
GROUPS = 32
TOKENS = MEMBERS * GROUPS
SHARES = 64
SHARE = 36
HELD = 40
ROWS = SHARES * SHARE + HELD - SHARE
STRIDE = 40
SCALE = 32**-0.5
LOG2E = math.log2(math.e)
NN = (((1,), (0,)), ((), ()))
NT = (((1,), (1,)), ((), ()))
TN = (((0,), (0,)), ((), ()))
CHIPS = ("zl", "x", "y", "zh")
VM = pl.BlockSpec(memory_space=pltpu.VMEM)
HBM = pl.BlockSpec(memory_space=pltpu.HBM)
MIB = 2**20


def dot(a, b, dims):
    return lax.dot_general(a, b, dims, preferred_element_type=F32)


def unpack(recv, refs):
    def step(s, _):
        for i, ref in enumerate(refs):
            first, lane = GROUPS * (i // 2), 128 * (i % 2)
            rows = recv[s, first : first + GROUPS, lane : lane + 128]
            ref[pl.ds(s * STRIDE, GROUPS), :] = rows.astype(F32)
        return 0

    lax.fori_loop(0, MEMBERS, step, 0, unroll=8)


def grouped(refs, first, count):
    columns = [
        jnp.concatenate(
            [ref[pl.ds(first + k, MEMBERS, stride=STRIDE), :] for k in range(count)], axis=0
        )
        for ref in refs
    ]
    return jnp.concatenate(columns, axis=1)


def normalise(x):
    centred = x - jnp.mean(x, -1, keepdims=True)
    inverse = lax.rsqrt(jnp.mean(centred * centred, -1, keepdims=True) + 1e-5)
    return centred * inverse, inverse


def head_masks():
    lane = lax.broadcasted_iota(jnp.int32, (MEMBERS, 128), 1) // 32
    return [lane == h for h in range(4)]


def expand(a, masks):
    zero = jnp.zeros_like(a)
    return jnp.concatenate([jnp.where(m, a, zero) for m in masks], axis=0)


def pick(r, masks):
    out = r[0:MEMBERS]
    for h in range(1, 4):
        out = jnp.where(masks[h], r[MEMBERS * h : MEMBERS * (h + 1)], out)
    return out


def attention(count, q, k, v, da, bias, masks):
    units = [(g, hf) for g in range(count) for hf in range(2)]

    def part(a, u):
        g, hf = u
        return a[MEMBERS * g : MEMBERS * (g + 1), 128 * hf : 128 * (hf + 1)]

    def diagonal(a, b):
        zero = jnp.zeros_like(a)
        top = jnp.concatenate([a, zero], axis=1)
        return jnp.concatenate([top, jnp.concatenate([zero, b], axis=1)], axis=0)

    wide = {}
    products = {}
    for u in units:
        wide[u] = jnp.concatenate([expand(part(q, u), masks), expand(part(da, u), masks)], axis=1)
        products[u] = dot(diagonal(part(k, u), part(v, u)), wide[u], NT)
    stacked = {}
    grad_bias = [None, None]
    for u in units:
        hf = u[1]
        logits = products[u][:MEMBERS] + bias[:, 256 * hf : 256 * (hf + 1)]
        grad_probs = products[u][MEMBERS:]
        e = jnp.exp2(logits - jnp.max(logits, 0, keepdims=True))
        p = e * (1.0 / jnp.sum(e, 0, keepdims=True))
        ds = p * (grad_probs - jnp.sum(grad_probs * p, 0, keepdims=True))
        stacked[u] = jnp.concatenate([p.astype(BF), ds.astype(BF)], axis=0)
        grad_bias[hf] = ds if grad_bias[hf] is None else grad_bias[hf] + ds
    results = {}
    for u in units:
        down = dot(stacked[u], wide[u], NN)
        grad_v = down[:MEMBERS, 128:]
        grad_k = down[MEMBERS:, :128] * (1.0 / LOG2E)
        across = dot(stacked[u], diagonal(part(v, u), part(k, u)), TN)
        attended = pick(across[:, :128], masks)
        grad_q = pick(across[:, 128:], masks) * SCALE
        results[u] = [r.astype(BF) for r in (attended, grad_q, grad_k, grad_v)]
    return results, grad_bias


def gradients_kernel(
    recv, gain, wqkv, wout, bias, msg, x0, x1, d0, d1, bias_t, grad_bias,
    normal_s, inverse_s, normed_s, q_s, k_s, v_s, da_s, dy_s, att_s, gp_s, rows_s,
):
    unpack(recv, (x0, x1, d0, d1))
    for t in range(4):
        bias_t[:, 128 * t : 128 * (t + 1)] = (bias[128 * t : 128 * (t + 1), :] * LOG2E).T
    grad_bias[...] = jnp.zeros_like(grad_bias)
    masks = head_masks()

    def project(b, _):
        rows = pl.ds(pl.multiple_of(b * 512, 512), 512)
        dy = grouped((d0, d1), b * 8, 8).astype(BF)
        dy_s[rows, :] = dy
        da_s[rows, :] = dot(dy, wout[...], NT).astype(BF)
        normal, inverse = normalise(grouped((x0, x1), b * 8, 8))
        normal_s[rows, :] = normal
        inverse_s[rows, :] = jnp.broadcast_to(inverse, (512, 128))
        normed = (normal * gain[...]).astype(BF)
        normed_s[rows, :] = normed
        packed = dot(normed, wqkv[...], NN)
        q_s[rows, :] = (packed[:, :256] * (SCALE * LOG2E)).astype(BF)
        k_s[rows, :] = packed[:, 256:512].astype(BF)
        v_s[rows, :] = packed[:, 512:].astype(BF)
        return 0

    lax.fori_loop(0, GROUPS // 8, project, 0, unroll=4)

    def attend(b, _):
        rows = pl.ds(pl.multiple_of(b * 512, 512), 512)
        results, gb = attention(
            8, q_s[rows, :], k_s[rows, :], v_s[rows, :], da_s[rows, :], bias_t, masks
        )
        for (g, hf), (att, gq, gk, gv) in results.items():
            r = pl.ds(pl.multiple_of(b * 512 + MEMBERS * g, MEMBERS), MEMBERS)
            att_s[r, 128 * hf : 128 * (hf + 1)] = att
            for i, part in enumerate((gq, gk, gv)):
                gp_s[r, 256 * i + 128 * hf : 256 * i + 128 * (hf + 1)] = part
        for hf in range(2):
            grad_bias[:, 256 * hf : 256 * (hf + 1)] += gb[hf]
        return 0

    lax.fori_loop(0, GROUPS // 8, attend, 0, unroll=4)
    def pull_back(b, _):
        rows = pl.ds(pl.multiple_of(b * 1024, 1024), 1024)
        g = dot(gp_s[rows, :], wqkv[...], NT) * gain[...]
        normal = normal_s[rows, :]
        inverse = jnp.concatenate([inverse_s[rows, :]] * 2, axis=1)
        along = jnp.mean(g * normal, -1, keepdims=True)
        dx = inverse * (g - jnp.mean(g, -1, keepdims=True) - normal * along)
        dx = dy_s[rows, :].astype(F32) + dx
        for k in range(16):
            for i, ref in enumerate((x0, x1)):
                ref[pl.ds(b * 16 + k, MEMBERS, stride=STRIDE), :] = dx[
                    MEMBERS * k : MEMBERS * (k + 1), 128 * i : 128 * (i + 1)
                ]
        return 0

    lax.fori_loop(0, GROUPS // 16, pull_back, 0, unroll=2)

    grad_qkv = dot(normed_s[...], gp_s[...], TN)
    grad_proj = dot(att_s[...], dy_s[...], TN)
    for t in range(6):
        rows_s[256 * t : 256 * (t + 1), :] = grad_qkv[:, 128 * t : 128 * (t + 1)]
    for t in range(2):
        rows_s[256 * (6 + t) : 256 * (7 + t), :] = grad_proj[:, 128 * t : 128 * (t + 1)]
    for t in range(4):
        rows_s[2048 + 64 * t : 2112 + 64 * t, :] = grad_bias[:, 128 * t : 128 * (t + 1)]
    rows_s[SHARES * SHARE :, :] = jnp.zeros((HELD - SHARE, 128), F32)
    for d in range(SHARES):
        msg[d, 2 * GROUPS :, :] = rows_s[SHARE * d : SHARE * d + HELD, :].astype(BF)

    def write(s, _):
        for i, ref in enumerate((x0, x1)):
            msg[s, GROUPS * i : GROUPS * (i + 1), :] = ref[pl.ds(s * STRIDE, GROUPS), :].astype(BF)
        return 0

    lax.fori_loop(0, MEMBERS, write, 0, unroll=8)


def gradients(recv, gain, wqkv, wout, bias):
    return pl.pallas_call(
        gradients_kernel,
        out_shape=jax.ShapeDtypeStruct((MEMBERS, 2 * GROUPS + HELD, 128), BF),
        in_specs=[VM] * 5,
        out_specs=VM,
        scratch_shapes=[
            *[pltpu.VMEM((MEMBERS * STRIDE, 128), F32)] * 4,
            *[pltpu.VMEM((MEMBERS, 512), F32)] * 2,
            pltpu.VMEM((TOKENS, 256), F32),
            pltpu.VMEM((TOKENS, 128), F32),
            *[pltpu.VMEM((TOKENS, 256), BF)] * 7,
            pltpu.VMEM((TOKENS, 768), BF),
            pltpu.VMEM((ROWS, 128), F32),
        ],
        compiler_params=pltpu.CompilerParams(vmem_limit_bytes=40 * MIB),
        name="layer_gradients",
    )(recv, gain, wqkv, wout, bias)


def finish_kernel(y, sums, gain, wqkv, dx, qkv, proj, bias, ggain, rows_s, weight, sem):
    copy = pltpu.make_async_copy(wqkv, weight, sem)
    copy.start()

    def step(s, _):
        dx[s, :, 0:128] = y[s, 0:32, :]
        dx[s, :, 128:256] = y[s, 32:64, :]
        return 0

    lax.fori_loop(0, 64, step, 0, unroll=8)
    for d in range(SHARES):
        share = sums[d].astype(F32)
        row = SHARE * d
        while row < SHARE * (d + 1):
            t, r = divmod(row, 256)
            count = min(256 - r, SHARE * (d + 1) - row)
            part = share[row - SHARE * d : row - SHARE * d + count]
            if t < 6:
                qkv[r : r + count, 128 * t : 128 * (t + 1)] = part
            elif t < 8:
                proj[r : r + count, 128 * (t - 6) : 128 * (t - 5)] = part
            else:
                rows_s[r : r + count, :] = part
            row += count
    for t in range(4):
        bias[128 * t : 128 * (t + 1), :] = rows_s[64 * t : 64 * (t + 1), :].T
    copy.wait()
    along = jnp.sum(qkv[...] * weight[...].astype(F32), -1, keepdims=True)
    ggain[...] = jnp.broadcast_to(along, (256, 128)).T[0:1] / gain[...]


def finish(y, sums, gain, wqkv):
    return pl.pallas_call(
        finish_kernel,
        out_shape=(
            jax.ShapeDtypeStruct((64, 32, 256), BF),
            jax.ShapeDtypeStruct((256, 768), F32),
            jax.ShapeDtypeStruct((256, 256), F32),
            jax.ShapeDtypeStruct((512, 64), F32),
            jax.ShapeDtypeStruct((1, 256), F32),
        ),
        in_specs=[VM, VM, VM, HBM],
        out_specs=(VM,) * 5,
        scratch_shapes=[
            pltpu.VMEM((256, 128), F32),
            pltpu.VMEM((256, 768), BF),
            pltpu.SemaphoreType.DMA,
        ],
        compiler_params=pltpu.CompilerParams(vmem_limit_bytes=12 * MIB),
        name="place_results",
    )(y, sums, gain, wqkv)


def on_device(activations, cotangent, ln_gain, qkv_weight, out_weight, position_bias):
    both = jnp.concatenate(
        [activations.reshape(64, 32, 256), cotangent.reshape(64, 32, 256)], axis=1
    )
    arrived = lax.all_to_all(both, CHIPS, 0, 0, tiled=True)
    gain = ln_gain.reshape(1, 256)
    message = gradients(arrived, gain, qkv_weight, out_weight, position_bias.reshape(512, 64))
    returned = lax.all_to_all(message, CHIPS, 0, 0, tiled=True)
    mine = jnp.sum(returned[:, 2 * GROUPS :, :].astype(F32), axis=0)
    other = lax.ppermute(mine, "core", [(0, 1), (1, 0)])
    total = jnp.broadcast_to((mine + other).astype(BF), (SHARES, HELD, 128))
    sums = lax.all_to_all(total, CHIPS, 0, 0, tiled=True)
    dx, grad_qkv, grad_proj, grad_bias, grad_gain = finish(returned, sums, gain, qkv_weight)
    return (
        dx.reshape(activations.shape),
        grad_gain.reshape(256),
        grad_qkv,
        grad_proj,
        grad_bias.reshape(8, 64, 64),
    )


def solution(mesh):
    fine = jax.sharding.Mesh(mesh.devices.reshape(2, 4, 4, 2, 2), (*CHIPS, "core"))
    tokens = P(None, ("zl", "x"), ("y", "zh", "core"), None)
    return jax.shard_map(
        on_device,
        mesh=fine,
        in_specs=(tokens, tokens, P(), P(), P(), P()),
        out_specs=(tokens, P(), P(), P(), P()),
        check_vma=False,
    )
```

```python
import functools
import math

import jax
import jax.numpy as jnp
from jax import lax
from jax.experimental import pallas as pl
from jax.experimental.pallas import tpu as pltpu
from jax.sharding import PartitionSpec as P

F32 = jnp.float32
BF = jnp.bfloat16
MEMBERS = 64
GROUPS = 32
TOKENS = MEMBERS * GROUPS
SHARES = 64
SHARE = 36
HELD = 40
ROWS = SHARES * SHARE + HELD - SHARE
STRIDE = 40
SCALE = 32**-0.5
LOG2E = math.log2(math.e)
NN = (((1,), (0,)), ((), ()))
NT = (((1,), (1,)), ((), ()))
TN = (((0,), (0,)), ((), ()))
CHIPS = ("zl", "x", "y", "zh")
VM = pl.BlockSpec(memory_space=pltpu.VMEM)
HBM = pl.BlockSpec(memory_space=pltpu.HBM)
MIB = 2**20


def dot(a, b, dims):
    return lax.dot_general(a, b, dims, preferred_element_type=F32)


def unpack(recv, refs):
    def step(s, _):
        for i, ref in enumerate(refs):
            first, lane = GROUPS * (i // 2), 128 * (i % 2)
            rows = recv[s, first : first + GROUPS, lane : lane + 128]
            ref[pl.ds(s * STRIDE, GROUPS), :] = rows.astype(F32)
        return 0

    lax.fori_loop(0, MEMBERS, step, 0, unroll=8)


def grouped(refs, first, count):
    columns = [
        jnp.concatenate(
            [ref[pl.ds(first + k, MEMBERS, stride=STRIDE), :] for k in range(count)], axis=0
        )
        for ref in refs
    ]
    return jnp.concatenate(columns, axis=1)


def normalise(x):
    centred = x - jnp.mean(x, -1, keepdims=True)
    inverse = lax.rsqrt(jnp.mean(centred * centred, -1, keepdims=True) + 1e-5)
    return centred * inverse, inverse


def head_masks():
    lane = lax.broadcasted_iota(jnp.int32, (MEMBERS, 128), 1) // 32
    return [lane == h for h in range(4)]


def expand(a, masks):
    zero = jnp.zeros_like(a)
    return jnp.concatenate([jnp.where(m, a, zero) for m in masks], axis=0)


def pick(r, masks):
    out = r[0:MEMBERS]
    for h in range(1, 4):
        out = jnp.where(masks[h], r[MEMBERS * h : MEMBERS * (h + 1)], out)
    return out


def attention(count, q, k, v, da, bias, masks):
    units = [(g, hf) for g in range(count) for hf in range(2)]

    def part(a, u):
        g, hf = u
        return a[MEMBERS * g : MEMBERS * (g + 1), 128 * hf : 128 * (hf + 1)]

    def diagonal(a, b):
        zero = jnp.zeros_like(a)
        top = jnp.concatenate([a, zero], axis=1)
        return jnp.concatenate([top, jnp.concatenate([zero, b], axis=1)], axis=0)

    wide = {}
    products = {}
    for u in units:
        wide[u] = jnp.concatenate([expand(part(q, u), masks), expand(part(da, u), masks)], axis=1)
        products[u] = dot(diagonal(part(k, u), part(v, u)), wide[u], NT)
    stacked = {}
    grad_bias = [None, None]
    for u in units:
        hf = u[1]
        logits = products[u][:MEMBERS] + bias[:, 256 * hf : 256 * (hf + 1)]
        grad_probs = products[u][MEMBERS:]
        e = jnp.exp2(logits - jnp.max(logits, 0, keepdims=True))
        p = e * (1.0 / jnp.sum(e, 0, keepdims=True))
        ds = p * (grad_probs - jnp.sum(grad_probs * p, 0, keepdims=True))
        stacked[u] = jnp.concatenate([p.astype(BF), ds.astype(BF)], axis=0)
        grad_bias[hf] = ds if grad_bias[hf] is None else grad_bias[hf] + ds
    results = {}
    for u in units:
        down = dot(stacked[u], wide[u], NN)
        grad_v = down[:MEMBERS, 128:]
        grad_k = down[MEMBERS:, :128] * (1.0 / LOG2E)
        across = dot(stacked[u], diagonal(part(v, u), part(k, u)), TN)
        attended = pick(across[:, :128], masks)
        grad_q = pick(across[:, 128:], masks) * SCALE
        results[u] = [r.astype(BF) for r in (attended, grad_q, grad_k, grad_v)]
    return results, grad_bias


def gradients_kernel(
    recv, gain, wqkv, wout, bias, msg, x0, x1, d0, d1, bias_t, grad_bias,
    normal_s, inverse_s, normed_s, q_s, k_s, v_s, da_s, dy_s, att_s, gp_s, rows_s,
):
    unpack(recv, (x0, x1, d0, d1))
    for t in range(4):
        bias_t[:, 128 * t : 128 * (t + 1)] = (bias[128 * t : 128 * (t + 1), :] * LOG2E).T
    grad_bias[...] = jnp.zeros_like(grad_bias)
    masks = head_masks()

    def project(b, _):
        rows = pl.ds(pl.multiple_of(b * 512, 512), 512)
        dy = grouped((d0, d1), b * 8, 8).astype(BF)
        dy_s[rows, :] = dy
        da_s[rows, :] = dot(dy, wout[...], NT).astype(BF)
        normal, inverse = normalise(grouped((x0, x1), b * 8, 8))
        normal_s[rows, :] = normal
        inverse_s[rows, :] = jnp.broadcast_to(inverse, (512, 128))
        normed = (normal * gain[...]).astype(BF)
        normed_s[rows, :] = normed
        packed = dot(normed, wqkv[...], NN)
        q_s[rows, :] = (packed[:, :256] * (SCALE * LOG2E)).astype(BF)
        k_s[rows, :] = packed[:, 256:512].astype(BF)
        v_s[rows, :] = packed[:, 512:].astype(BF)
        return 0

    lax.fori_loop(0, GROUPS // 8, project, 0, unroll=4)

    def attend(b, _):
        rows = pl.ds(pl.multiple_of(b * 512, 512), 512)
        results, gb = attention(
            8, q_s[rows, :], k_s[rows, :], v_s[rows, :], da_s[rows, :], bias_t, masks
        )
        for (g, hf), (att, gq, gk, gv) in results.items():
            r = pl.ds(pl.multiple_of(b * 512 + MEMBERS * g, MEMBERS), MEMBERS)
            att_s[r, 128 * hf : 128 * (hf + 1)] = att
            for i, part in enumerate((gq, gk, gv)):
                gp_s[r, 256 * i + 128 * hf : 256 * i + 128 * (hf + 1)] = part
        for hf in range(2):
            grad_bias[:, 256 * hf : 256 * (hf + 1)] += gb[hf]
        return 0

    lax.fori_loop(0, GROUPS // 8, attend, 0, unroll=4)
    def pull_back(b, _):
        rows = pl.ds(pl.multiple_of(b * 512, 512), 512)
        g = dot(gp_s[rows, :], wqkv[...], NT) * gain[...]
        normal = normal_s[rows, :]
        inverse = jnp.concatenate([inverse_s[rows, :]] * 2, axis=1)
        along = jnp.mean(g * normal, -1, keepdims=True)
        dx = inverse * (g - jnp.mean(g, -1, keepdims=True) - normal * along)
        dx = dy_s[rows, :].astype(F32) + dx
        for k in range(8):
            for i, ref in enumerate((x0, x1)):
                ref[pl.ds(b * 8 + k, MEMBERS, stride=STRIDE), :] = dx[
                    MEMBERS * k : MEMBERS * (k + 1), 128 * i : 128 * (i + 1)
                ]
        return 0

    lax.fori_loop(0, GROUPS // 8, pull_back, 0, unroll=4)

    grad_qkv = dot(normed_s[...], gp_s[...], TN)
    grad_proj = dot(att_s[...], dy_s[...], TN)
    for t in range(6):
        rows_s[256 * t : 256 * (t + 1), :] = grad_qkv[:, 128 * t : 128 * (t + 1)]
    for t in range(2):
        rows_s[256 * (6 + t) : 256 * (7 + t), :] = grad_proj[:, 128 * t : 128 * (t + 1)]
    for t in range(4):
        rows_s[2048 + 64 * t : 2112 + 64 * t, :] = grad_bias[:, 128 * t : 128 * (t + 1)]
    rows_s[SHARES * SHARE :, :] = jnp.zeros((HELD - SHARE, 128), F32)
    for d in range(SHARES):
        msg[d, 2 * GROUPS :, :] = rows_s[SHARE * d : SHARE * d + HELD, :].astype(BF)

    def write(s, _):
        for i, ref in enumerate((x0, x1)):
            msg[s, GROUPS * i : GROUPS * (i + 1), :] = ref[pl.ds(s * STRIDE, GROUPS), :].astype(BF)
        return 0

    lax.fori_loop(0, MEMBERS, write, 0, unroll=8)


def gradients(recv, gain, wqkv, wout, bias):
    return pl.pallas_call(
        gradients_kernel,
        out_shape=jax.ShapeDtypeStruct((MEMBERS, 2 * GROUPS + HELD, 128), BF),
        in_specs=[VM] * 5,
        out_specs=VM,
        scratch_shapes=[
            *[pltpu.VMEM((MEMBERS * STRIDE, 128), F32)] * 4,
            *[pltpu.VMEM((MEMBERS, 512), F32)] * 2,
            pltpu.VMEM((TOKENS, 256), F32),
            pltpu.VMEM((TOKENS, 128), F32),
            *[pltpu.VMEM((TOKENS, 256), BF)] * 7,
            pltpu.VMEM((TOKENS, 768), BF),
            pltpu.VMEM((ROWS, 128), F32),
        ],
        compiler_params=pltpu.CompilerParams(vmem_limit_bytes=40 * MIB),
        name="layer_gradients",
    )(recv, gain, wqkv, wout, bias)


def finish_kernel(y, sums, gain, wqkv, dx, qkv, proj, bias, ggain, rows_s, weight, sem):
    copy = pltpu.make_async_copy(wqkv, weight, sem)
    copy.start()

    def step(s, _):
        dx[s, :, 0:128] = y[s, 0:32, :]
        dx[s, :, 128:256] = y[s, 32:64, :]
        return 0

    lax.fori_loop(0, 64, step, 0, unroll=64)
    for d in range(SHARES):
        share = sums[d].astype(F32)
        row = SHARE * d
        while row < SHARE * (d + 1):
            t, r = divmod(row, 256)
            count = min(256 - r, SHARE * (d + 1) - row)
            part = share[row - SHARE * d : row - SHARE * d + count]
            if t < 6:
                qkv[r : r + count, 128 * t : 128 * (t + 1)] = part
            elif t < 8:
                proj[r : r + count, 128 * (t - 6) : 128 * (t - 5)] = part
            else:
                rows_s[r : r + count, :] = part
            row += count
    for t in range(4):
        bias[128 * t : 128 * (t + 1), :] = rows_s[64 * t : 64 * (t + 1), :].T
    copy.wait()
    along = jnp.sum(qkv[...] * weight[...].astype(F32), -1, keepdims=True)
    ggain[...] = jnp.broadcast_to(along, (256, 128)).T[0:1] / gain[...]


def finish(y, sums, gain, wqkv):
    return pl.pallas_call(
        finish_kernel,
        out_shape=(
            jax.ShapeDtypeStruct((64, 32, 256), BF),
            jax.ShapeDtypeStruct((256, 768), F32),
            jax.ShapeDtypeStruct((256, 256), F32),
            jax.ShapeDtypeStruct((512, 64), F32),
            jax.ShapeDtypeStruct((1, 256), F32),
        ),
        in_specs=[VM, VM, VM, HBM],
        out_specs=(VM,) * 5,
        scratch_shapes=[
            pltpu.VMEM((256, 128), F32),
            pltpu.VMEM((256, 768), BF),
            pltpu.SemaphoreType.DMA,
        ],
        compiler_params=pltpu.CompilerParams(vmem_limit_bytes=12 * MIB),
        name="place_results",
    )(y, sums, gain, wqkv)


def on_device(activations, cotangent, ln_gain, qkv_weight, out_weight, position_bias):
    both = jnp.concatenate(
        [activations.reshape(64, 32, 256), cotangent.reshape(64, 32, 256)], axis=1
    )
    arrived = lax.all_to_all(both, CHIPS, 0, 0, tiled=True)
    gain = ln_gain.reshape(1, 256)
    message = gradients(arrived, gain, qkv_weight, out_weight, position_bias.reshape(512, 64))
    returned = lax.all_to_all(message, CHIPS, 0, 0, tiled=True)
    mine = jnp.sum(returned[:, 2 * GROUPS :, :].astype(F32), axis=0)
    other = lax.ppermute(mine, "core", [(0, 1), (1, 0)])
    total = jnp.broadcast_to((mine + other).astype(BF), (SHARES, HELD, 128))
    sums = lax.all_to_all(total, CHIPS, 0, 0, tiled=True)
    dx, grad_qkv, grad_proj, grad_bias, grad_gain = finish(returned, sums, gain, qkv_weight)
    return (
        dx.reshape(activations.shape),
        grad_gain.reshape(256),
        grad_qkv,
        grad_proj,
        grad_bias.reshape(8, 64, 64),
    )


def solution(mesh):
    fine = jax.sharding.Mesh(mesh.devices.reshape(2, 4, 4, 2, 2), (*CHIPS, "core"))
    tokens = P(None, ("zl", "x"), ("y", "zh", "core"), None)
    return jax.shard_map(
        on_device,
        mesh=fine,
        in_specs=(tokens, tokens, P(), P(), P(), P()),
        out_specs=(tokens, P(), P(), P(), P()),
        check_vma=False,
    )
```
